32 devices in a mesh: seq: 8 (over y, x, core), tp: 4 (over z).
Axes of the slice: x: 2, y: 2, z: 4, core: 2. Of those that a mesh axis runs over, the one named last changes fastest.
Arguments:
- codes: bfloat16 [4096, 4096], P('seq', 'tp'), may hold values from -127 to 127, as said below
- exponents: int32 [4096], P('seq'), may hold values from -8 to -5
- w_query: bfloat16 [4096, 4096], P(None, 'tp'), may hold values from -0.09375 to 0.09375
- w_key: bfloat16 [4096, 4096], P(None, 'tp'), may hold values from -0.09375 to 0.09375
- w_value: bfloat16 [4096, 4096], P(None, 'tp'), may hold values from -0.09375 to 0.09375
- norm_gain: float32 [4096], P('tp'), may hold values from 0.1 to 1.9
- w_out: bfloat16 [4096, 4096], P('tp'), may hold values from -0.09375 to 0.09375
Outputs:
- mixed: bfloat16 [4096, 4096], P(('seq', 'tp'))
The draws below stay inside these ranges and needn't reach their ends.
Inputs may be any that keep to these rules, and one draw needn't show every extreme that they name: `codes`: every entry is a whole number.
All inputs are finite; a program needn't handle non-finite values.
Results may differ from the reference program's by a relative error of at most 0.012.
Values may be sent and summed in bfloat16 or wider, within the bound.
A program may use at most 128 MiB of HBM per device.

```python
import jax
import jax.numpy as jnp
from jax import lax

D = 4096
H = 32
HD = 128
BLK = 512
TOKENS = 4096


def draw_codes(key, part):
    whole = jax.random.randint(key, (TOKENS, D), -127, 128)
    return whole.astype(jnp.float32).astype(jnp.bfloat16)


def touch_ends(drawn, stream_key, least, top_value):
    spot = [jax.random.randint(jax.random.fold_in(stream_key, axis), (), 0, length) for axis, length in enumerate(drawn.shape)]
    main_axis = drawn.shape.index(max(drawn.shape))
    beside = spot[:main_axis] + [(spot[main_axis] + 1) % drawn.shape[main_axis]] + spot[main_axis + 1:]
    return drawn.at[tuple(spot)].set(least).at[tuple(beside)].set(top_value)


def level_of(rng, dims, cuts, least, largest):
    level, own = 1.0, jax.random.fold_in(rng, 6)
    for axis_at, shards_of in cuts:
        steps = jnp.exp(jax.random.uniform(jax.random.fold_in(own, axis_at), (shards_of,), jnp.float32, least / len(cuts), largest / len(cuts)))
        level = level * jnp.repeat(steps, dims[axis_at] // shards_of).reshape([-1 if axis == axis_at else 1 for axis in range(len(dims))])
    return level


def bell_draw(rng, dims, spread, limit, split=(), held_as=jnp.bfloat16):
    entries = jax.random.normal(rng, dims, jnp.float32) * spread
    if len(split) > 0:
        entries = level_of(rng, dims, split, -0.22, 0.18) * entries
    return jnp.clip(entries, min=-limit, max=limit).astype(held_as)


def setup_inputs(seed: int = 0) -> dict:
    keys = jax.random.split(jax.random.key(seed), 8)
    return {
        "codes": draw_codes(jax.random.fold_in(keys[7], 71), 0),
        "exponents": touch_ends(jax.random.randint(keys[1], (TOKENS,), -8, -4), jax.random.fold_in(keys[1], 1), -8, (-4) - 1).astype(jnp.int32),
        "w_query": bell_draw(keys[2], (D, H * HD), D ** -0.5, 0.09375, ((1, 4),)),
        "w_key": bell_draw(keys[3], (D, H * HD), D ** -0.5, 0.09375, ((1, 4),)),
        "w_value": bell_draw(keys[4], (D, H * HD), D ** -0.5, 0.09375, ((1, 4),)),
        "norm_gain": jnp.clip(1.0 + 0.18 * jax.random.normal(keys[5], (H * HD,), jnp.float32), 0.1, 1.9),
        "w_out": bell_draw(keys[6], (H * HD, D), (H * HD) ** -0.5, 0.09375, ((0, 4),)),
    }


def reference(codes, exponents, w_query, w_key, w_value, norm_gain, w_out):
    blocks = codes.shape[0] // BLK
    causal = jnp.tril(jnp.ones((BLK, BLK), jnp.float32))
    gain = norm_gain.reshape(H, HD)

    def step(state, index):
        start = (index * BLK).astype(jnp.int32)
        block_codes = lax.dynamic_slice_in_dim(codes, start, BLK, 0).astype(jnp.float32)
        block_exps = lax.dynamic_slice_in_dim(exponents, start, BLK, 0).astype(jnp.float32)
        x = (block_codes * jnp.exp2(block_exps)[:, None]).astype(jnp.bfloat16)
        q = jnp.dot(x, w_query, preferred_element_type=jnp.float32)
        k = jnp.dot(x, w_key, preferred_element_type=jnp.float32)
        v = jnp.dot(x, w_value, preferred_element_type=jnp.float32)
        feat_q = (jax.nn.elu(q) + 1.0).astype(jnp.bfloat16).astype(jnp.float32).reshape(BLK, H, HD)
        feat_k = (jax.nn.elu(k) + 1.0).astype(jnp.bfloat16).astype(jnp.float32).reshape(BLK, H, HD)
        values = v.astype(jnp.bfloat16).astype(jnp.float32).reshape(BLK, H, HD)
        state_b = state.astype(jnp.bfloat16).astype(jnp.float32)
        inter = jnp.einsum('shd,hde->she', feat_q, state_b, precision=lax.Precision.HIGHEST)
        scores = jnp.einsum('shd,thd->hst', feat_q, feat_k, precision=lax.Precision.HIGHEST) * causal[None]
        scores = scores.astype(jnp.bfloat16).astype(jnp.float32)
        intra = jnp.einsum('hst,the->she', scores, values, precision=lax.Precision.HIGHEST)
        y = inter + intra
        mean_sq = lax.optimization_barrier(jnp.mean(y * y, axis=-1, keepdims=True))
        normed = (y * lax.rsqrt(mean_sq + 1e-05) * gain[None]).astype(jnp.bfloat16).reshape(BLK, H * HD)
        out = jnp.dot(normed, w_out, preferred_element_type=jnp.float32).astype(jnp.bfloat16)
        state = state + jnp.einsum('shd,she->hde', feat_k, values, precision=lax.Precision.HIGHEST)
        return (state, out)
    init = jnp.zeros((H, HD, HD), jnp.float32)
    final, outs = lax.scan(step, init, jnp.arange(blocks, dtype=jnp.int32))
    return outs.reshape(blocks * BLK, w_out.shape[1])
```

```python
import functools

import jax
import jax.numpy as jnp
from jax import lax
from jax.experimental import pallas as pl
from jax.experimental.pallas import tpu as pltpu
from jax.sharding import PartitionSpec as P

HD = 128
MESH = pl.DeviceIdType.MESH
GATHER_CHUNKS = 4
OUT_CHUNKS = 8
BF = jnp.bfloat16
F32 = jnp.float32


def feature(t):
    return jnp.where(t > 0, t + 1.0, jnp.exp(jnp.minimum(t, 0.0)))


def kernel(
    n, seqs, x_ref, wq_ref, wk_ref, wv_ref, gain_ref, wo_ref, out_ref,
    xg, w, wo, acc, tot, pre, sbuf, rbuf, part, land,
    x_sem, w_sem, wo_sem, g_send, g_recv, s_send, s_recv, r_send, r_recv,
):
    z = lax.axis_index("tp")
    s = lax.axis_index("seq")
    toks, feats = xg.shape[1], xg.shape[2]
    width = acc.shape[2]
    heads = width // HD
    rows = toks // n
    ow = part.shape[2]
    outs = part.shape[0]
    crows = toks // GATHER_CHUNKS
    steps = seqs.bit_length() - 1

    def partner(i):
        d = 1 << i
        return s + d * (1 - 2 * ((s // d) % 2))

    own = pltpu.make_async_copy(x_ref, xg.at[z], x_sem)
    own.start()

    def w_copy(m, b):
        src = (wq_ref, wk_ref, wv_ref)[m]
        block = pl.ds(pl.multiple_of(b * feats, feats), feats)
        return pltpu.make_async_copy(src.at[block], w.at[m, block], w_sem.at[m, b])

    def each_block(t, fn):
        if t == 0:
            fn(z)
            return
        pl.when(z - t >= 0)(lambda: fn(z - t))
        pl.when(z + t < n)(lambda: fn(z + t))

    def start_w(b):
        for m in range(3):
            w_copy(m, b).start()

    start_w(z)

    barrier = pltpu.get_barrier_semaphore()
    for i in range(steps):
        pl.semaphore_signal(barrier, inc=1, device_id={"seq": partner(i)}, device_id_type=MESH)

    @pl.when(z > 0)
    def _():
        pl.semaphore_signal(barrier, inc=1, device_id={"tp": z - 1}, device_id_type=MESH)

    @pl.when(z < n - 1)
    def _():
        pl.semaphore_signal(barrier, inc=1, device_id={"tp": z + 1}, device_id_type=MESH)

    near = jnp.where(z > 0, 1, 0) + jnp.where(z < n - 1, 1, 0)
    pl.semaphore_wait(barrier, near + steps)

    def g_copy(b, c, up):
        chunk = xg.at[b, pl.ds(c * crows, crows)]
        return pltpu.make_async_remote_copy(
            src_ref=chunk, dst_ref=chunk,
            send_sem=g_send.at[0 if up else 1, b, c], recv_sem=g_recv.at[b, c],
            device_id={"tp": z + 1 if up else z - 1}, device_id_type=MESH,
        )

    def pass_on(b, c, up):
        if up:
            pl.when(z < n - 1)(lambda: g_copy(b, c, True).start())
        else:
            pl.when(z > 0)(lambda: g_copy(b, c, False).start())

    own.wait()
    for c in range(GATHER_CHUNKS):
        pass_on(z, c, True)
        pass_on(z, c, False)

    for t in range(1, n):
        each_block(t, start_w)
    wo_copy = pltpu.make_async_copy(wo_ref, wo, wo_sem)
    wo_copy.start()

    tile = min(256, width)

    def project(b, m, first):
        w_copy(m, b).wait()
        block = pl.ds(pl.multiple_of(b * feats, feats), feats)

        @pl.loop(0, width // tile)
        def _(j):
            cols = pl.ds(pl.multiple_of(j * tile, tile), tile)
            term = jnp.dot(xg[b], w[m, block, cols], preferred_element_type=F32)
            if first:
                acc[m, :, cols] = term
            else:
                acc[m, :, cols] += term

    def project_all(first):
        def go(b):
            for m in (1, 2, 0):
                project(b, m, first)
        return go

    project_all(True)(z)
    for t in range(1, n):
        for c in range(GATHER_CHUNKS):
            @pl.when(z - t >= 0)
            def _():
                g_copy(z - t, c, True).wait_recv()
                pass_on(z - t, c, True)

            @pl.when(z + t < n)
            def _():
                g_copy(z + t, c, False).wait_recv()
                pass_on(z + t, c, False)
        each_block(t, project_all(False))

    for t in range(n):
        for c in range(GATHER_CHUNKS):
            @pl.when((z - t >= 0) & (z < n - 1))
            def _():
                g_copy(z - t, c, True).wait_send()

            @pl.when((z + t < n) & (z > 0))
            def _():
                g_copy(z + t, c, False).wait_send()

    fk, vb, fq, o = xg.at[0], xg.at[1], xg.at[2], xg.at[3]

    def head(h):
        return pl.ds(pl.multiple_of(h * HD, HD), HD)

    @pl.loop(0, heads)
    def _(h):
        cols = head(h)
        key = feature(acc[1, :, cols]).astype(BF)
        val = acc[2, :, cols].astype(BF)
        fk[:, cols] = key
        vb[:, cols] = val
        tot[cols, :] = lax.dot_general(key, val, (((0,), (0,)), ((), ())), preferred_element_type=F32)

    pre[...] = jnp.zeros_like(pre)
    at_or_before = lax.broadcasted_iota(jnp.int32, (toks, toks), 0) >= lax.broadcasted_iota(
        jnp.int32, (toks, toks), 1
    )

    def intra(h):
        cols = head(h)
        qry = feature(acc[0, :, cols]).astype(BF)
        fq[:, cols] = qry
        scores = lax.dot_general(qry, fk[:, cols], (((1,), (1,)), ((), ())), preferred_element_type=F32)
        scores = jnp.where(at_or_before, scores, 0.0).astype(BF)
        acc[0, :, cols] = jnp.dot(scores, vb[:, cols], preferred_element_type=F32)

    def s_copy(i):
        return pltpu.make_async_remote_copy(
            src_ref=sbuf.at[i], dst_ref=rbuf.at[i], send_sem=s_send.at[i], recv_sem=s_recv.at[i],
            device_id={"seq": partner(i)}, device_id_type=MESH,
        )

    for i in range(steps):
        sbuf[i] = tot[...].astype(BF)
        s_copy(i).start()
        pl.loop(i * heads // steps, (i + 1) * heads // steps)(intra)
        s_copy(i).wait()
        came = rbuf[i].astype(F32)
        tot[...] += came

        @pl.when((s // (1 << i)) % 2 == 1)
        def _():
            pre[...] += came

    @pl.loop(0, heads)
    def _(h):
        cols = head(h)
        y = acc[0, :, cols] + jnp.dot(fq[:, cols], pre[cols, :].astype(BF), preferred_element_type=F32)
        mean_sq = jnp.mean(y * y, axis=-1, keepdims=True)
        o[:, cols] = (y * lax.rsqrt(mean_sq + 1e-05) * gain_ref[:, cols]).astype(BF)

    wo_copy.wait()

    def r_copy(c, j, up):
        src = part.at[c, pl.ds(j * rows, rows)]
        slot = j if up else jnp.where(z - 1 == j, n, j)
        return pltpu.make_async_remote_copy(
            src_ref=src, dst_ref=land.at[slot, c],
            send_sem=r_send.at[j, c], recv_sem=r_recv.at[slot, c],
            device_id={"tp": z + 1 if up else z - 1}, device_id_type=MESH,
        )

    def arrived(c, slot):
        ref = land.at[slot, c]
        pltpu.make_async_copy(ref, ref, r_recv.at[slot, c]).wait()
        return land[slot, c].astype(F32)

    def add_landed(c, j):
        mine = pl.ds(j * rows, rows)
        part[c, mine, :] = (part[c, mine, :].astype(F32) + arrived(c, j)).astype(BF)

    @pl.loop(0, outs)
    def _(c):
        cols = pl.ds(pl.multiple_of(c * ow, ow), ow)
        part[c] = jnp.dot(o[...], wo[:, cols], preferred_element_type=F32).astype(BF)
        for k in range(n - 1):
            up_j, down_j = n - 1 - k, k

            @pl.when(z < up_j)
            def _():
                pl.when(z > 0)(lambda: add_landed(c, up_j))
                r_copy(c, up_j, True).start()

            @pl.when(z > down_j)
            def _():
                pl.when(z < n - 1)(lambda: add_landed(c, down_j))
                r_copy(c, down_j, False).start()

    @pl.loop(0, outs)
    def _(c):
        cols = pl.ds(pl.multiple_of(c * ow, ow), ow)
        mine = pl.ds(pl.multiple_of(z * rows, rows), rows)
        total = part[c, mine, :].astype(F32)

        @pl.when(z == 0)
        def _():
            out_ref[:, cols] = (total + arrived(c, n)).astype(BF)

        @pl.when(z == n - 1)
        def _():
            out_ref[:, cols] = (total + arrived(c, n - 1)).astype(BF)

        @pl.when((z > 0) & (z < n - 1))
        def _():
            out_ref[:, cols] = (total + arrived(c, z) + arrived(c, n)).astype(BF)

    @pl.loop(0, outs)
    def _(c):
        for j in range(n):
            pl.when(z < j)(lambda: r_copy(c, j, True).wait_send())
            pl.when(z > j)(lambda: r_copy(c, j, False).wait_send())


def on_device(n, seqs, codes, exponents, w_query, w_key, w_value, norm_gain, w_out):
    toks, feats = codes.shape
    depth, width = w_query.shape
    model = w_out.shape[1]
    rows = toks // n
    ow = model // OUT_CHUNKS
    steps = seqs.bit_length() - 1
    x = (codes.astype(F32) * jnp.exp2(exponents.astype(F32))[:, None]).astype(BF)
    hbm = pl.BlockSpec(memory_space=pl.ANY)
    vmem = pl.BlockSpec(memory_space=pltpu.VMEM)
    dma = pltpu.SemaphoreType.DMA
    return pl.pallas_call(
        functools.partial(kernel, n, seqs),
        out_shape=jax.ShapeDtypeStruct((rows, model), BF),
        in_specs=[hbm, hbm, hbm, hbm, vmem, hbm],
        out_specs=vmem,
        scratch_shapes=[
            pltpu.VMEM((n, toks, feats), BF),
            pltpu.VMEM((3, depth, width), BF),
            pltpu.VMEM((width, model), BF),
            pltpu.VMEM((3, toks, width), F32),
            pltpu.VMEM((width, HD), F32),
            pltpu.VMEM((width, HD), F32),
            pltpu.VMEM((steps, width, HD), BF),
            pltpu.VMEM((steps, width, HD), BF),
            pltpu.VMEM((OUT_CHUNKS, toks, ow), BF),
            pltpu.VMEM((n + 1, OUT_CHUNKS, rows, ow), BF),
            dma(()),
            dma((3, n)),
            dma(()),
            dma((2, n, GATHER_CHUNKS)),
            dma((n, GATHER_CHUNKS)),
            dma((steps,)),
            dma((steps,)),
            dma((n, OUT_CHUNKS)),
            dma((n + 1, OUT_CHUNKS)),
        ],
        compiler_params=pltpu.CompilerParams(
            collective_id=0, has_side_effects=True, vmem_limit_bytes=62 * 1024 * 1024
        ),
        cost_estimate=pl.CostEstimate(
            flops=2 * toks * width * (3 * depth + model) + 4 * toks * toks * width,
            bytes_accessed=2 * (3 * depth * width + width * model),
            transcendentals=2 * toks * width,
        ),
    )(x, w_query, w_key, w_value, norm_gain.reshape(1, width), w_out)


def solution(mesh):
    in_specs = (
        P("seq", "tp"), P("seq"), P(None, "tp"), P(None, "tp"), P(None, "tp"), P("tp"), P("tp", None),
    )
    body = functools.partial(on_device, mesh.shape["tp"], mesh.shape["seq"])
    return jax.shard_map(
        body, mesh=mesh, in_specs=in_specs, out_specs=P(("seq", "tp"), None), check_vma=False
    )
```

```python
import functools

import jax
import jax.numpy as jnp
from jax import lax
from jax.experimental import pallas as pl
from jax.experimental.pallas import tpu as pltpu
from jax.sharding import PartitionSpec as P

HD = 128
MESH = pl.DeviceIdType.MESH
GATHER_CHUNKS = 4
OUT_CHUNKS = 8
WINDOW = 2
BF = jnp.bfloat16
F32 = jnp.float32


def feature(t):
    return jnp.where(t > 0, t + 1.0, jnp.exp(jnp.minimum(t, 0.0)))


def kernel(
    n, seqs, x_ref, exp_ref, wq_ref, wk_ref, wv_ref, gain_ref, wo_ref, out_ref,
    xg, w, wo, acc, scale, tot, pre, sbuf, rbuf, part, land,
    x_sem, w_sem, wo_sem, g_send, g_recv, s_send, s_recv, r_send, r_recv,
):
    z = lax.axis_index("tp")
    s = lax.axis_index("seq")
    toks, feats = xg.shape[1], xg.shape[2]
    width = acc.shape[2]
    heads = width // HD
    rows = toks // n
    ow = part.shape[2]
    outs = part.shape[0]
    crows = toks // GATHER_CHUNKS
    steps = seqs.bit_length() - 1

    def partner(i):
        d = 1 << i
        return s + d * (1 - 2 * ((s // d) % 2))

    own = pltpu.make_async_copy(x_ref, xg.at[z], x_sem)
    own.start()

    def w_copy(m, b):
        src = (wq_ref, wk_ref, wv_ref)[m]
        block = pl.ds(pl.multiple_of(b * feats, feats), feats)
        return pltpu.make_async_copy(src.at[block], w.at[m, block], w_sem.at[m, b])

    def each_block(t, fn):
        if t == 0:
            fn(z)
            return
        pl.when(z - t >= 0)(lambda: fn(z - t))
        pl.when(z + t < n)(lambda: fn(z + t))

    def start_w(b):
        for m in range(3):
            w_copy(m, b).start()

    start_w(z)

    barrier = pltpu.get_barrier_semaphore()
    for i in range(steps):
        pl.semaphore_signal(barrier, inc=1, device_id={"seq": partner(i)}, device_id_type=MESH)

    @pl.when(z > 0)
    def _():
        pl.semaphore_signal(barrier, inc=1, device_id={"tp": z - 1}, device_id_type=MESH)

    @pl.when(z < n - 1)
    def _():
        pl.semaphore_signal(barrier, inc=1, device_id={"tp": z + 1}, device_id_type=MESH)

    near = jnp.where(z > 0, 1, 0) + jnp.where(z < n - 1, 1, 0)
    pl.semaphore_wait(barrier, near + steps)

    def g_copy(b, c, up):
        chunk = xg.at[b, pl.ds(c * crows, crows)]
        return pltpu.make_async_remote_copy(
            src_ref=chunk, dst_ref=chunk,
            send_sem=g_send.at[0 if up else 1, b, c], recv_sem=g_recv.at[b, c],
            device_id={"tp": z + 1 if up else z - 1}, device_id_type=MESH,
        )

    def pass_on(b, c, up):
        if up:
            pl.when(z < n - 1)(lambda: g_copy(b, c, True).start())
        else:
            pl.when(z > 0)(lambda: g_copy(b, c, False).start())

    own.wait()
    for c in range(GATHER_CHUNKS):
        pass_on(z, c, True)
        pass_on(z, c, False)

    for t in range(1, n):
        each_block(t, start_w)
    wo_copy = pltpu.make_async_copy(wo_ref, wo, wo_sem)
    wo_copy.start()

    on_diagonal = lax.broadcasted_iota(jnp.int32, (toks, toks), 0) == lax.broadcasted_iota(
        jnp.int32, (toks, toks), 1
    )
    row_scale = jnp.where(on_diagonal, jnp.exp2(exp_ref[...].astype(F32)), 0.0)
    scale[...] = jnp.broadcast_to(jnp.sum(row_scale, axis=1, keepdims=True), scale.shape)

    tile = min(256, width)

    def project(b, m, first):
        w_copy(m, b).wait()
        block = pl.ds(pl.multiple_of(b * feats, feats), feats)

        @pl.loop(0, width // tile)
        def _(j):
            cols = pl.ds(pl.multiple_of(j * tile, tile), tile)
            term = jnp.dot(xg[b], w[m, block, cols], preferred_element_type=F32)
            if first:
                acc[m, :, cols] = term
            else:
                acc[m, :, cols] += term

    def project_all(first):
        def go(b):
            for m in (1, 2, 0):
                project(b, m, first)
        return go

    project_all(True)(z)
    for t in range(1, n):
        for c in range(GATHER_CHUNKS):
            @pl.when(z - t >= 0)
            def _():
                g_copy(z - t, c, True).wait_recv()
                pass_on(z - t, c, True)

            @pl.when(z + t < n)
            def _():
                g_copy(z + t, c, False).wait_recv()
                pass_on(z + t, c, False)
        each_block(t, project_all(False))

    for t in range(n):
        for c in range(GATHER_CHUNKS):
            @pl.when((z - t >= 0) & (z < n - 1))
            def _():
                g_copy(z - t, c, True).wait_send()

            @pl.when((z + t < n) & (z > 0))
            def _():
                g_copy(z + t, c, False).wait_send()

    fk, vb, fq, o = xg.at[0], xg.at[1], xg.at[2], xg.at[3]

    def head(h):
        return pl.ds(pl.multiple_of(h * HD, HD), HD)

    @pl.loop(0, heads)
    def _(h):
        cols = head(h)
        key = feature(acc[1, :, cols] * scale[...]).astype(BF)
        val = (acc[2, :, cols] * scale[...]).astype(BF)
        fk[:, cols] = key
        vb[:, cols] = val
        tot[cols, :] = lax.dot_general(key, val, (((0,), (0,)), ((), ())), preferred_element_type=F32)

    pre[...] = jnp.zeros_like(pre)
    at_or_before = lax.broadcasted_iota(jnp.int32, (toks, toks), 0) >= lax.broadcasted_iota(
        jnp.int32, (toks, toks), 1
    )

    def intra(h):
        cols = head(h)
        qry = feature(acc[0, :, cols] * scale[...]).astype(BF)
        fq[:, cols] = qry
        scores = lax.dot_general(qry, fk[:, cols], (((1,), (1,)), ((), ())), preferred_element_type=F32)
        scores = jnp.where(at_or_before, scores, 0.0).astype(BF)
        acc[0, :, cols] = jnp.dot(scores, vb[:, cols], preferred_element_type=F32)

    def s_copy(i):
        return pltpu.make_async_remote_copy(
            src_ref=sbuf.at[i], dst_ref=rbuf.at[i], send_sem=s_send.at[i], recv_sem=s_recv.at[i],
            device_id={"seq": partner(i)}, device_id_type=MESH,
        )

    for i in range(steps):
        sbuf[i] = tot[...].astype(BF)
        s_copy(i).start()
        pl.loop(i * heads // steps, (i + 1) * heads // steps)(intra)
        s_copy(i).wait()
        came = rbuf[i].astype(F32)
        tot[...] += came

        @pl.when((s // (1 << i)) % 2 == 1)
        def _():
            pre[...] += came

    @pl.loop(0, heads)
    def _(h):
        cols = head(h)
        y = acc[0, :, cols] + jnp.dot(fq[:, cols], pre[cols, :].astype(BF), preferred_element_type=F32)
        mean_sq = jnp.mean(y * y, axis=-1, keepdims=True)
        o[:, cols] = (y * lax.rsqrt(mean_sq + 1e-05) * gain_ref[:, cols]).astype(BF)

    wo_copy.wait()

    def r_copy(c, j, up):
        src = part.at[c, pl.ds(j * rows, rows)]
        slot = j if up else jnp.where(z - 1 == j, n, j)
        return pltpu.make_async_remote_copy(
            src_ref=src, dst_ref=land.at[slot, c],
            send_sem=r_send.at[j, c], recv_sem=r_recv.at[slot, c],
            device_id={"tp": z + 1 if up else z - 1}, device_id_type=MESH,
        )

    def arrived(c, slot):
        ref = land.at[slot, c]
        pltpu.make_async_copy(ref, ref, r_recv.at[slot, c]).wait()
        return land[slot, c].astype(F32)

    def add_landed(c, j):
        mine = pl.ds(j * rows, rows)
        part[c, mine, :] = (part[c, mine, :].astype(F32) + arrived(c, j)).astype(BF)

    def sent(c):
        for j in range(n):
            pl.when(z < j)(lambda: r_copy(c, j, True).wait_send())
            pl.when(z > j)(lambda: r_copy(c, j, False).wait_send())

    @pl.loop(0, outs)
    def _(c):
        cols = pl.ds(pl.multiple_of(c * ow, ow), ow)
        part[c] = jnp.dot(o[...], wo[:, cols], preferred_element_type=F32).astype(BF)
        pl.when(c >= WINDOW)(lambda: sent(c - WINDOW))
        for k in range(n - 1):
            up_j, down_j = n - 1 - k, k

            @pl.when(z < up_j)
            def _():
                pl.when(z > 0)(lambda: add_landed(c, up_j))
                r_copy(c, up_j, True).start()

            @pl.when(z > down_j)
            def _():
                pl.when(z < n - 1)(lambda: add_landed(c, down_j))
                r_copy(c, down_j, False).start()

    @pl.loop(0, outs)
    def _(c):
        cols = pl.ds(pl.multiple_of(c * ow, ow), ow)
        mine = pl.ds(pl.multiple_of(z * rows, rows), rows)
        total = part[c, mine, :].astype(F32)

        @pl.when(z == 0)
        def _():
            out_ref[:, cols] = (total + arrived(c, n)).astype(BF)

        @pl.when(z == n - 1)
        def _():
            out_ref[:, cols] = (total + arrived(c, n - 1)).astype(BF)

        @pl.when((z > 0) & (z < n - 1))
        def _():
            out_ref[:, cols] = (total + arrived(c, z) + arrived(c, n)).astype(BF)

    pl.loop(outs - WINDOW, outs)(sent)


def on_device(n, seqs, codes, exponents, w_query, w_key, w_value, norm_gain, w_out):
    toks, feats = codes.shape
    depth, width = w_query.shape
    model = w_out.shape[1]
    rows = toks // n
    ow = model // OUT_CHUNKS
    steps = seqs.bit_length() - 1
    hbm = pl.BlockSpec(memory_space=pl.ANY)
    vmem = pl.BlockSpec(memory_space=pltpu.VMEM)
    dma = pltpu.SemaphoreType.DMA
    return pl.pallas_call(
        functools.partial(kernel, n, seqs),
        out_shape=jax.ShapeDtypeStruct((rows, model), BF),
        in_specs=[hbm, vmem, hbm, hbm, hbm, vmem, hbm],
        out_specs=vmem,
        scratch_shapes=[
            pltpu.VMEM((n, toks, feats), BF),
            pltpu.VMEM((3, depth, width), BF),
            pltpu.VMEM((width, model), BF),
            pltpu.VMEM((3, toks, width), F32),
            pltpu.VMEM((toks, HD), F32),
            pltpu.VMEM((width, HD), F32),
            pltpu.VMEM((width, HD), F32),
            pltpu.VMEM((steps, width, HD), BF),
            pltpu.VMEM((steps, width, HD), BF),
            pltpu.VMEM((OUT_CHUNKS, toks, ow), BF),
            pltpu.VMEM((n + 1, OUT_CHUNKS, rows, ow), BF),
            dma(()),
            dma((3, n)),
            dma(()),
            dma((2, n, GATHER_CHUNKS)),
            dma((n, GATHER_CHUNKS)),
            dma((steps,)),
            dma((steps,)),
            dma((n, OUT_CHUNKS)),
            dma((n + 1, OUT_CHUNKS)),
        ],
        compiler_params=pltpu.CompilerParams(
            collective_id=0, has_side_effects=True, vmem_limit_bytes=62 * 1024 * 1024
        ),
        cost_estimate=pl.CostEstimate(
            flops=2 * toks * width * (3 * depth + model) + 4 * toks * toks * width,
            bytes_accessed=2 * (3 * depth * width + width * model),
            transcendentals=2 * toks * width,
        ),
    )(codes, exponents.reshape(1, toks), w_query, w_key, w_value, norm_gain.reshape(1, width), w_out)


def solution(mesh):
    in_specs = (
        P("seq", "tp"), P("seq"), P(None, "tp"), P(None, "tp"), P(None, "tp"), P("tp"), P("tp", None),
    )
    body = functools.partial(on_device, mesh.shape["tp"], mesh.shape["seq"])
    return jax.shard_map(
        body, mesh=mesh, in_specs=in_specs, out_specs=P(("seq", "tp"), None), check_vma=False
    )
```

```python
import functools

import jax
import jax.numpy as jnp
from jax import lax
from jax.experimental import pallas as pl
from jax.experimental.pallas import tpu as pltpu
from jax.sharding import PartitionSpec as P

HD = 128
MESH = pl.DeviceIdType.MESH
GATHER_CHUNKS = 4
OUT_CHUNKS = 8
BF = jnp.bfloat16
F32 = jnp.float32


def feature(t):
    return jnp.where(t > 0, t + 1.0, jnp.exp(jnp.minimum(t, 0.0)))


def kernel(
    n, seqs, x_ref, exp_ref, wq_ref, wk_ref, wv_ref, gain_ref, wo_ref, out_ref, far,
    xg, w, wo, acc, scale, tot, pre, sbuf, rbuf, part, land,
    x_sem, w_sem, wo_sem, g_send, g_recv, s_send, s_recv, r_send, r_recv,
    f_send, f_recv, b_send, b_recv, t_send, t_recv, far_sem,
):
    z = lax.axis_index("tp")
    s = lax.axis_index("seq")
    toks, feats = xg.shape[1], xg.shape[2]
    width = acc.shape[2]
    heads = width // HD
    rows = toks // n
    ow = part.shape[2]
    outs = part.shape[0]
    crows = toks // GATHER_CHUNKS
    steps = seqs.bit_length() - 1
    half = seqs // 2
    mine_k, core = s // 2, s % 2
    slice_rows = width // seqs
    slice_cols = wo.shape[1] // GATHER_CHUNKS
    donor = (z == 0) | (z == n - 1)
    helper = (z == 1) | (z == n - 2)

    def partner(i):
        d = 1 << i
        return s + d * (1 - 2 * ((s // d) % 2))

    own = pltpu.make_async_copy(x_ref, xg.at[z], x_sem)
    own.start()

    def w_copy(m, b):
        src = (wq_ref, wk_ref, wv_ref)[m]
        block = pl.ds(pl.multiple_of(b * feats, feats), feats)
        return pltpu.make_async_copy(src.at[block], w.at[m, block], w_sem.at[m, b])

    def each_block(t, fn):
        if t == 0:
            fn(z)
            return
        pl.when(z - t >= 0)(lambda: fn(z - t))
        pl.when(z + t < n)(lambda: fn(z + t))

    def start_w(b):
        for m in range(3):
            w_copy(m, b).start()

    start_w(z)

    barrier = pltpu.get_barrier_semaphore()
    for i in range(steps):
        pl.semaphore_signal(barrier, inc=1, device_id={"seq": partner(i)}, device_id_type=MESH)

    @pl.loop(0, half)
    def _(k):
        @pl.when(k != mine_k)
        def _():
            pl.semaphore_signal(barrier, inc=1, device_id={"seq": 2 * k + core}, device_id_type=MESH)

    @pl.when(z > 0)
    def _():
        pl.semaphore_signal(barrier, inc=1, device_id={"tp": z - 1}, device_id_type=MESH)

    @pl.when(z < n - 1)
    def _():
        pl.semaphore_signal(barrier, inc=1, device_id={"tp": z + 1}, device_id_type=MESH)

    near = jnp.where(z > 0, 1, 0) + jnp.where(z < n - 1, 1, 0)
    pl.semaphore_wait(barrier, near + steps + half - 1)

    def g_copy(b, c, up):
        chunk = xg.at[b, pl.ds(c * crows, crows)]
        return pltpu.make_async_remote_copy(
            src_ref=chunk, dst_ref=chunk,
            send_sem=g_send.at[0 if up else 1, b, c], recv_sem=g_recv.at[b, c],
            device_id={"tp": z + 1 if up else z - 1}, device_id_type=MESH,
        )

    def pass_on(b, c, up):
        if up:
            pl.when(z < n - 1)(lambda: g_copy(b, c, True).start())
        else:
            pl.when(z > 0)(lambda: g_copy(b, c, False).start())

    own.wait()
    for c in range(GATHER_CHUNKS):
        pass_on(z, c, True)
        pass_on(z, c, False)

    for t in range(1, n):
        each_block(t, start_w)
    wo_copy = pltpu.make_async_copy(wo_ref, wo, wo_sem)
    wo_copy.start()

    on_diagonal = lax.broadcasted_iota(jnp.int32, (toks, toks), 0) == lax.broadcasted_iota(
        jnp.int32, (toks, toks), 1
    )
    row_scale = jnp.where(on_diagonal, jnp.exp2(exp_ref[...].astype(F32)), 0.0)
    scale[...] = jnp.broadcast_to(jnp.sum(row_scale, axis=1, keepdims=True), scale.shape)

    tile = min(256, width)

    def project(b, m, first):
        w_copy(m, b).wait()
        block = pl.ds(pl.multiple_of(b * feats, feats), feats)

        @pl.loop(0, width // tile)
        def _(j):
            cols = pl.ds(pl.multiple_of(j * tile, tile), tile)
            term = jnp.dot(xg[b], w[m, block, cols], preferred_element_type=F32)
            if first:
                acc[m, :, cols] = term
            else:
                acc[m, :, cols] += term

    def project_all(first):
        def go(b):
            for m in (1, 2, 0):
                project(b, m, first)
        return go

    def slice_of(ref, q, c):
        at = pl.ds(pl.multiple_of(q * slice_rows, slice_rows), slice_rows)
        return ref.at[at] if c is None else ref.at[at, pl.ds(c * slice_cols, slice_cols)]

    def hand_in(c):
        return pltpu.make_async_remote_copy(
            src_ref=slice_of(wo_ref, s, c), dst_ref=slice_of(far, s, c),
            send_sem=f_send.at[c], recv_sem=f_recv.at[c],
            device_id={"tp": jnp.where(z == 0, 1, n - 2)}, device_id_type=MESH,
        )

    def spread(k, c):
        return pltpu.make_async_remote_copy(
            src_ref=slice_of(far, s, c), dst_ref=slice_of(far, s, c),
            send_sem=b_send.at[k, c], recv_sem=b_recv.at[mine_k, c],
            device_id={"seq": 2 * k + core}, device_id_type=MESH,
        )

    def spread_came(k, c):
        piece = slice_of(far, 2 * k + core, c)
        pltpu.make_async_copy(piece, piece, b_recv.at[k, c]).wait()

    def to_twin(k):
        piece = slice_of(far, 2 * k + core, None)
        return pltpu.make_async_remote_copy(
            src_ref=piece, dst_ref=piece, send_sem=t_send.at[k], recv_sem=t_recv.at[k],
            device_id={"seq": partner(0)}, device_id_type=MESH,
        )

    def others(fn):
        @pl.loop(0, half)
        def _(k):
            pl.when(k != mine_k)(lambda: fn(k))

    def spread_slice(c):
        hand_in(c).wait_recv()
        others(lambda k: spread(k, c).start())

    project_all(True)(z)
    for t in range(1, n):
        if t == 2:
            @pl.when(donor)
            def _():
                for c in range(GATHER_CHUNKS):
                    hand_in(c).start()

        for c in range(GATHER_CHUNKS):
            if t == 2:
                pl.when(helper & (c > 0))(lambda: spread_slice(c - 1))

            @pl.when(z - t >= 0)
            def _():
                g_copy(z - t, c, True).wait_recv()
                pass_on(z - t, c, True)

            @pl.when(z + t < n)
            def _():
                g_copy(z + t, c, False).wait_recv()
                pass_on(z + t, c, False)
        if t == 2:
            pl.when(helper)(lambda: spread_slice(GATHER_CHUNKS - 1))
        each_block(t, project_all(False))

    for t in range(n):
        for c in range(GATHER_CHUNKS):
            @pl.when((z - t >= 0) & (z < n - 1))
            def _():
                g_copy(z - t, c, True).wait_send()

            @pl.when((z + t < n) & (z > 0))
            def _():
                g_copy(z + t, c, False).wait_send()

    fk, vb, fq, o = xg.at[0], xg.at[1], xg.at[2], xg.at[3]

    def head(h):
        return pl.ds(pl.multiple_of(h * HD, HD), HD)

    @pl.loop(0, heads)
    def _(h):
        cols = head(h)
        key = feature(acc[1, :, cols] * scale[...]).astype(BF)
        val = (acc[2, :, cols] * scale[...]).astype(BF)
        fk[:, cols] = key
        vb[:, cols] = val
        tot[cols, :] = lax.dot_general(key, val, (((0,), (0,)), ((), ())), preferred_element_type=F32)

    pre[...] = jnp.zeros_like(pre)
    at_or_before = lax.broadcasted_iota(jnp.int32, (toks, toks), 0) >= lax.broadcasted_iota(
        jnp.int32, (toks, toks), 1
    )

    def intra(h):
        cols = head(h)
        qry = feature(acc[0, :, cols] * scale[...]).astype(BF)
        fq[:, cols] = qry
        scores = lax.dot_general(qry, fk[:, cols], (((1,), (1,)), ((), ())), preferred_element_type=F32)
        scores = jnp.where(at_or_before, scores, 0.0).astype(BF)
        acc[0, :, cols] = jnp.dot(scores, vb[:, cols], preferred_element_type=F32)

    def s_copy(i):
        return pltpu.make_async_remote_copy(
            src_ref=sbuf.at[i], dst_ref=rbuf.at[i], send_sem=s_send.at[i], recv_sem=s_recv.at[i],
            device_id={"seq": partner(i)}, device_id_type=MESH,
        )

    for i in range(steps):
        sbuf[i] = tot[...].astype(BF)
        s_copy(i).start()
        pl.loop(i * heads // steps, (i + 1) * heads // steps)(intra)
        s_copy(i).wait()
        came = rbuf[i].astype(F32)
        tot[...] += came

        @pl.when((s // (1 << i)) % 2 == 1)
        def _():
            pre[...] += came

    @pl.loop(0, heads)
    def _(h):
        cols = head(h)
        y = acc[0, :, cols] + jnp.dot(fq[:, cols], pre[cols, :].astype(BF), preferred_element_type=F32)
        mean_sq = jnp.mean(y * y, axis=-1, keepdims=True)
        o[:, cols] = (y * lax.rsqrt(mean_sq + 1e-05) * gain_ref[:, cols]).astype(BF)

    wo_copy.wait()

    def far_copy(b):
        return pltpu.make_async_copy(
            far.at[:, pl.ds(b * width, width)], w.at[0, pl.ds(b * width, width)], far_sem.at[b]
        )

    blocks = wo.shape[1] // width
    pieces = width // ow

    def r_copy(c, j, up, pre_norm=None):
        src = part.at[c, pl.ds(j * rows, rows)]
        if pre_norm is not None:
            src = pre_norm.at[pl.ds(j * rows, rows), pl.ds(c * ow, ow)]
        slot = j if up else jnp.where(z - 1 == j, n, j)
        return pltpu.make_async_remote_copy(
            src_ref=src, dst_ref=land.at[slot, c],
            send_sem=r_send.at[j, c], recv_sem=r_recv.at[slot, c],
            device_id={"tp": z + 1 if up else z - 1}, device_id_type=MESH,
        )

    for k in range(n - 1):
        for p in range(pieces):
            pl.when(z == 0)(lambda: r_copy(p, n - 1 - k, True, o).start())
            pl.when(z == n - 1)(lambda: r_copy(p, k, False, o).start())

    @pl.when(helper)
    def _():
        @pl.loop(0, half)
        def _(k):
            @pl.when(k != mine_k)
            def _():
                for c in range(GATHER_CHUNKS):
                    spread_came(k, c)
            to_twin(k).start()

        @pl.loop(0, half)
        def _(k):
            piece = slice_of(far, 2 * k + 1 - core, None)
            pltpu.make_async_copy(piece, piece, t_recv.at[k]).wait()

        for b in range(blocks):
            far_copy(b).start()
        for b in range(blocks):
            far_copy(b).wait()

    def landed(c, slot):
        ref = land.at[slot, c]
        pltpu.make_async_copy(ref, ref, r_recv.at[slot, c]).wait()

    def arrived(c, slot):
        landed(c, slot)
        return land[slot, c].astype(F32)

    def add_landed(c, j):
        mine = pl.ds(j * rows, rows)
        part[c, mine, :] = (part[c, mine, :].astype(F32) + arrived(c, j)).astype(BF)

    def outer_term(c, slot):
        total = jnp.zeros((rows, ow), F32)
        for p in range(pieces):
            at = pl.ds(pl.multiple_of((c // pieces) * width + p * ow, ow), ow)
            cols = pl.ds(pl.multiple_of((c % pieces) * ow, ow), ow)
            total += jnp.dot(land[slot, p], w[0, at, cols], preferred_element_type=F32)
        return total

    def add_outer(c, j):
        mine = pl.ds(j * rows, rows)
        part[c, mine, :] = (part[c, mine, :].astype(F32) + outer_term(c, j)).astype(BF)

    @pl.loop(0, outs)
    def _(c):
        cols = pl.ds(pl.multiple_of(c * ow, ow), ow)
        part[c] = jnp.dot(o[...], wo[:, cols], preferred_element_type=F32).astype(BF)

    for k in range(n - 2):
        up_j, down_j = n - 1 - k, k

        @pl.when(z == 1)
        def _():
            for p in range(pieces):
                landed(p, up_j)

        @pl.when(z == n - 2)
        def _():
            for p in range(pieces):
                landed(p, down_j)

        @pl.loop(0, outs)
        def _(c):
            @pl.when((z < up_j) & (z > 0))
            def _():
                pl.when(z > 1)(lambda: add_landed(c, up_j))
                pl.when(z == 1)(lambda: add_outer(c, up_j))
                r_copy(c, up_j, True).start()

            @pl.when((z > down_j) & (z < n - 1))
            def _():
                pl.when(z < n - 2)(lambda: add_landed(c, down_j))
                pl.when(z == n - 2)(lambda: add_outer(c, down_j))
                r_copy(c, down_j, False).start()

    @pl.when(z == 1)
    def _():
        for p in range(pieces):
            landed(p, 1)

    @pl.when(z == n - 2)
    def _():
        for p in range(pieces):
            landed(p, n)

    @pl.loop(0, outs)
    def _(c):
        cols = pl.ds(pl.multiple_of(c * ow, ow), ow)
        mine = pl.ds(pl.multiple_of(z * rows, rows), rows)
        total = part[c, mine, :].astype(F32)

        @pl.when(z == 0)
        def _():
            out_ref[:, cols] = (total + arrived(c, n)).astype(BF)

        @pl.when(z == n - 1)
        def _():
            out_ref[:, cols] = (total + arrived(c, n - 1)).astype(BF)

        @pl.when(z == 1)
        def _():
            out_ref[:, cols] = (total + outer_term(c, 1) + arrived(c, n)).astype(BF)

        @pl.when(z == n - 2)
        def _():
            out_ref[:, cols] = (total + outer_term(c, n) + arrived(c, n - 2)).astype(BF)

        if n > 4:
            @pl.when((z > 1) & (z < n - 2))
            def _():
                out_ref[:, cols] = (total + arrived(c, z) + arrived(c, n)).astype(BF)

    @pl.loop(0, outs)
    def _(c):
        for j in range(n):
            pl.when((z < j) & (z > 0))(lambda: r_copy(c, j, True).wait_send())
            pl.when((z > j) & (z < n - 1))(lambda: r_copy(c, j, False).wait_send())

    for k in range(n - 1):
        for p in range(pieces):
            pl.when(z == 0)(lambda: r_copy(p, n - 1 - k, True, o).wait_send())
            pl.when(z == n - 1)(lambda: r_copy(p, k, False, o).wait_send())

    @pl.when(donor)
    def _():
        for c in range(GATHER_CHUNKS):
            hand_in(c).wait_send()

    @pl.when(helper)
    def _():
        @pl.loop(0, half)
        def _(k):
            @pl.when(k != mine_k)
            def _():
                for c in range(GATHER_CHUNKS):
                    spread(k, c).wait_send()
            to_twin(k).wait_send()


def on_device(n, seqs, codes, exponents, w_query, w_key, w_value, norm_gain, w_out):
    toks, feats = codes.shape
    depth, width = w_query.shape
    model = w_out.shape[1]
    rows = toks // n
    ow = model // OUT_CHUNKS
    steps = seqs.bit_length() - 1
    hbm = pl.BlockSpec(memory_space=pl.ANY)
    vmem = pl.BlockSpec(memory_space=pltpu.VMEM)
    dma = pltpu.SemaphoreType.DMA
    return pl.pallas_call(
        functools.partial(kernel, n, seqs),
        out_shape=(jax.ShapeDtypeStruct((rows, model), BF), jax.ShapeDtypeStruct((width, model), BF)),
        in_specs=[hbm, vmem, hbm, hbm, hbm, vmem, hbm],
        out_specs=(vmem, hbm),
        scratch_shapes=[
            pltpu.VMEM((n, toks, feats), BF),
            pltpu.VMEM((3, depth, width), BF),
            pltpu.VMEM((width, model), BF),
            pltpu.VMEM((3, toks, width), F32),
            pltpu.VMEM((toks, HD), F32),
            pltpu.VMEM((width, HD), F32),
            pltpu.VMEM((width, HD), F32),
            pltpu.VMEM((steps, width, HD), BF),
            pltpu.VMEM((steps, width, HD), BF),
            pltpu.VMEM((OUT_CHUNKS, toks, ow), BF),
            pltpu.VMEM((n + 1, OUT_CHUNKS, rows, ow), BF),
            dma(()),
            dma((3, n)),
            dma(()),
            dma((2, n, GATHER_CHUNKS)),
            dma((n, GATHER_CHUNKS)),
            dma((steps,)),
            dma((steps,)),
            dma((n, OUT_CHUNKS)),
            dma((n + 1, OUT_CHUNKS)),
            dma((GATHER_CHUNKS,)),
            dma((GATHER_CHUNKS,)),
            dma((seqs // 2, GATHER_CHUNKS)),
            dma((seqs // 2, GATHER_CHUNKS)),
            dma((seqs // 2,)),
            dma((seqs // 2,)),
            dma((model // width,)),
        ],
        compiler_params=pltpu.CompilerParams(
            collective_id=0, has_side_effects=True, vmem_limit_bytes=62 * 1024 * 1024
        ),
        cost_estimate=pl.CostEstimate(
            flops=2 * toks * width * (3 * depth + model) + 4 * toks * toks * width,
            bytes_accessed=2 * (3 * depth * width + width * model),
            transcendentals=2 * toks * width,
        ),
    )(codes, exponents.reshape(1, toks), w_query, w_key, w_value, norm_gain.reshape(1, width), w_out)[0]


def solution(mesh):
    in_specs = (
        P("seq", "tp"), P("seq"), P(None, "tp"), P(None, "tp"), P(None, "tp"), P("tp"), P("tp", None),
    )
    body = functools.partial(on_device, mesh.shape["tp"], mesh.shape["seq"])
    return jax.shard_map(
        body, mesh=mesh, in_specs=in_specs, out_specs=P(("seq", "tp"), None), check_vma=False
    )
```

```python
import functools

import jax
import jax.numpy as jnp
from jax import lax
from jax.experimental import pallas as pl
from jax.experimental.pallas import tpu as pltpu
from jax.sharding import PartitionSpec as P

HD = 128
MESH = pl.DeviceIdType.MESH
GATHER_CHUNKS = 4
OUT_CHUNKS = 8
BF = jnp.bfloat16
F32 = jnp.float32


def feature(t):
    return jnp.where(t > 0, t + 1.0, jnp.exp(jnp.minimum(t, 0.0)))


def kernel(
    n, seqs, x_ref, exp_ref, wq_ref, wk_ref, wv_ref, gain_ref, wo_ref, out_ref, far,
    xg, w, wo, acc, scale, tot, pre, sbuf, rbuf, part, land,
    x_sem, w_sem, wo_sem, g_send, g_recv, s_send, s_recv, r_send, r_recv,
    f_send, f_recv, b_send, b_recv, t_send, t_recv, far_sem,
):
    z = lax.axis_index("tp")
    s = lax.axis_index("seq")
    toks, feats = xg.shape[1], xg.shape[2]
    width = acc.shape[2]
    heads = width // HD
    rows = toks // n
    ow = part.shape[2]
    outs = part.shape[0]
    crows = toks // GATHER_CHUNKS
    steps = seqs.bit_length() - 1
    half = seqs // 2
    mine_k, core = s // 2, s % 2
    slice_rows = width // seqs
    slice_cols = wo.shape[1] // GATHER_CHUNKS
    donor = (z == 0) | (z == n - 1)
    helper = (z == 1) | (z == n - 2)

    def partner(i):
        d = 1 << i
        return s + d * (1 - 2 * ((s // d) % 2))

    own = pltpu.make_async_copy(x_ref, xg.at[z], x_sem)
    own.start()

    def w_copy(m, b):
        src = (wq_ref, wk_ref, wv_ref)[m]
        block = pl.ds(pl.multiple_of(b * feats, feats), feats)
        return pltpu.make_async_copy(src.at[block], w.at[m, block], w_sem.at[m, b])

    def from_below(t):
        late = (z == 1) if t == 2 else (z < 0)
        return ((z >= t) & (z != 1)) | late, jnp.where(z == 1, 0, z - t)

    def from_above(t):
        late = (z == n - 2) if t == 2 else (z < 0)
        return ((z + t < n) & (z != n - 2)) | late, jnp.where(z == n - 2, n - 1, z + t)

    def each_block(t, fn):
        if t == 0:
            fn(z)
            return
        pl.when(from_below(t)[0])(lambda: fn(from_below(t)[1]))
        pl.when(from_above(t)[0])(lambda: fn(from_above(t)[1]))

    def start_w(b):
        for m in range(3):
            w_copy(m, b).start()

    start_w(z)

    barrier = pltpu.get_barrier_semaphore()
    for i in range(steps):
        pl.semaphore_signal(barrier, inc=1, device_id={"seq": partner(i)}, device_id_type=MESH)

    @pl.loop(0, half)
    def _(k):
        @pl.when(k != mine_k)
        def _():
            pl.semaphore_signal(barrier, inc=1, device_id={"seq": 2 * k + core}, device_id_type=MESH)

    @pl.when(z > 0)
    def _():
        pl.semaphore_signal(barrier, inc=1, device_id={"tp": z - 1}, device_id_type=MESH)

    @pl.when(z < n - 1)
    def _():
        pl.semaphore_signal(barrier, inc=1, device_id={"tp": z + 1}, device_id_type=MESH)

    near = jnp.where(z > 0, 1, 0) + jnp.where(z < n - 1, 1, 0)
    pl.semaphore_wait(barrier, near + steps + half - 1)

    def g_copy(b, c, up):
        chunk = xg.at[b, pl.ds(c * crows, crows)]
        return pltpu.make_async_remote_copy(
            src_ref=chunk, dst_ref=chunk,
            send_sem=g_send.at[0 if up else 1, b, c], recv_sem=g_recv.at[b, c],
            device_id={"tp": z + 1 if up else z - 1}, device_id_type=MESH,
        )

    def pass_on(b, c, up):
        if up:
            pl.when(z < n - 1)(lambda: g_copy(b, c, True).start())
        else:
            pl.when(z > 0)(lambda: g_copy(b, c, False).start())

    def slice_of(ref, q, c):
        at = pl.ds(pl.multiple_of(q * slice_rows, slice_rows), slice_rows)
        return ref.at[at] if c is None else ref.at[at, pl.ds(c * slice_cols, slice_cols)]

    def hand_in(c):
        return pltpu.make_async_remote_copy(
            src_ref=slice_of(wo_ref, s, c), dst_ref=slice_of(far, s, c),
            send_sem=f_send.at[c], recv_sem=f_recv.at[c],
            device_id={"tp": jnp.where(z == 0, 1, n - 2)}, device_id_type=MESH,
        )

    def spread(k, c):
        return pltpu.make_async_remote_copy(
            src_ref=slice_of(far, s, c), dst_ref=slice_of(far, s, c),
            send_sem=b_send.at[k, c], recv_sem=b_recv.at[mine_k, c],
            device_id={"seq": 2 * k + core}, device_id_type=MESH,
        )

    def spread_came(k, c):
        piece = slice_of(far, 2 * k + core, c)
        pltpu.make_async_copy(piece, piece, b_recv.at[k, c]).wait()

    def to_twin(k):
        piece = slice_of(far, 2 * k + core, None)
        return pltpu.make_async_remote_copy(
            src_ref=piece, dst_ref=piece, send_sem=t_send.at[k], recv_sem=t_recv.at[k],
            device_id={"seq": partner(0)}, device_id_type=MESH,
        )

    def others(fn):
        @pl.loop(0, half)
        def _(k):
            pl.when(k != mine_k)(lambda: fn(k))

    def spread_slice(c):
        hand_in(c).wait_recv()
        others(lambda k: spread(k, c).start())

    def send_own(c):
        pass_on(z, c, True)
        pass_on(z, c, False)

    def own_sent(c):
        pl.when(z == 0)(lambda: g_copy(z, c, True).wait_send())
        pl.when(z == n - 1)(lambda: g_copy(z, c, False).wait_send())

    own.wait()

    @pl.when(donor)
    def _():
        for c in range(GATHER_CHUNKS):
            hand_in(c).start()

    @pl.when((z > 0) & (z < n - 1))
    def _():
        for c in range(GATHER_CHUNKS):
            send_own(c)

    for t in range(1, n):
        each_block(t, start_w)
    wo_copy = pltpu.make_async_copy(wo_ref, wo, wo_sem)
    wo_copy.start()

    on_diagonal = lax.broadcasted_iota(jnp.int32, (toks, toks), 0) == lax.broadcasted_iota(
        jnp.int32, (toks, toks), 1
    )
    row_scale = jnp.where(on_diagonal, jnp.exp2(exp_ref[...].astype(F32)), 0.0)
    scale[...] = jnp.broadcast_to(jnp.sum(row_scale, axis=1, keepdims=True), scale.shape)

    tile = min(256, width)

    def project(b, m, first):
        w_copy(m, b).wait()
        block = pl.ds(pl.multiple_of(b * feats, feats), feats)

        @pl.loop(0, width // tile)
        def _(j):
            cols = pl.ds(pl.multiple_of(j * tile, tile), tile)
            term = jnp.dot(xg[b], w[m, block, cols], preferred_element_type=F32)
            if first:
                acc[m, :, cols] = term
            else:
                acc[m, :, cols] += term

    def project_all(first):
        def go(b):
            for m in (1, 2, 0):
                project(b, m, first)
        return go

    project_all(True)(z)
    for t in range(1, n):
        if t == 2:
            @pl.when(donor)
            def _():
                for c in range(GATHER_CHUNKS):
                    own_sent(c)
                    if c + 2 < GATHER_CHUNKS:
                        send_own(c + 2)

        below, low = from_below(t)
        above, high = from_above(t)
        for c in range(GATHER_CHUNKS):
            @pl.when(below)
            def _():
                g_copy(low, c, True).wait_recv()
                pass_on(low, c, True)

            @pl.when(above)
            def _():
                g_copy(high, c, False).wait_recv()
                pass_on(high, c, False)

            if t == 1:
                pl.when(helper)(lambda: spread_slice(c))
        if t == 1:
            @pl.when(donor)
            def _():
                for c in range(GATHER_CHUNKS):
                    hand_in(c).wait_send()
                for c in range(2):
                    send_own(c)
        each_block(t, project_all(False))

    for c in range(GATHER_CHUNKS):
        @pl.when((z > 0) & (z < n - 1))
        def _():
            g_copy(z, c, True).wait_send()
            g_copy(z, c, False).wait_send()

        for t in range(1, n):
            pl.when(from_below(t)[0] & (z < n - 1))(lambda: g_copy(from_below(t)[1], c, True).wait_send())
            pl.when(from_above(t)[0] & (z > 0))(lambda: g_copy(from_above(t)[1], c, False).wait_send())

    fk, vb, fq, o = xg.at[0], xg.at[1], xg.at[2], xg.at[3]

    def head(h):
        return pl.ds(pl.multiple_of(h * HD, HD), HD)

    @pl.loop(0, heads)
    def _(h):
        cols = head(h)
        key = feature(acc[1, :, cols] * scale[...]).astype(BF)
        val = (acc[2, :, cols] * scale[...]).astype(BF)
        fk[:, cols] = key
        vb[:, cols] = val
        tot[cols, :] = lax.dot_general(key, val, (((0,), (0,)), ((), ())), preferred_element_type=F32)

    pre[...] = jnp.zeros_like(pre)
    at_or_before = lax.broadcasted_iota(jnp.int32, (toks, toks), 0) >= lax.broadcasted_iota(
        jnp.int32, (toks, toks), 1
    )

    def intra(h):
        cols = head(h)
        qry = feature(acc[0, :, cols] * scale[...]).astype(BF)
        fq[:, cols] = qry
        scores = lax.dot_general(qry, fk[:, cols], (((1,), (1,)), ((), ())), preferred_element_type=F32)
        scores = jnp.where(at_or_before, scores, 0.0).astype(BF)
        acc[0, :, cols] = jnp.dot(scores, vb[:, cols], preferred_element_type=F32)

    def s_copy(i):
        return pltpu.make_async_remote_copy(
            src_ref=sbuf.at[i], dst_ref=rbuf.at[i], send_sem=s_send.at[i], recv_sem=s_recv.at[i],
            device_id={"seq": partner(i)}, device_id_type=MESH,
        )

    for i in range(steps):
        sbuf[i] = tot[...].astype(BF)
        s_copy(i).start()
        pl.loop(i * heads // steps, (i + 1) * heads // steps)(intra)
        s_copy(i).wait()
        came = rbuf[i].astype(F32)
        tot[...] += came

        @pl.when((s // (1 << i)) % 2 == 1)
        def _():
            pre[...] += came

    @pl.loop(0, heads)
    def _(h):
        cols = head(h)
        y = acc[0, :, cols] + jnp.dot(fq[:, cols], pre[cols, :].astype(BF), preferred_element_type=F32)
        mean_sq = jnp.mean(y * y, axis=-1, keepdims=True)
        o[:, cols] = (y * lax.rsqrt(mean_sq + 1e-05) * gain_ref[:, cols]).astype(BF)

    wo_copy.wait()

    def far_copy(b):
        return pltpu.make_async_copy(
            far.at[:, pl.ds(b * width, width)], w.at[0, pl.ds(b * width, width)], far_sem.at[b]
        )

    blocks = wo.shape[1] // width
    pieces = width // ow

    def r_copy(c, j, up, pre_norm=None):
        src = part.at[c, pl.ds(j * rows, rows)]
        if pre_norm is not None:
            src = pre_norm.at[pl.ds(j * rows, rows), pl.ds(c * ow, ow)]
        slot = j if up else jnp.where(z - 1 == j, n, j)
        return pltpu.make_async_remote_copy(
            src_ref=src, dst_ref=land.at[slot, c],
            send_sem=r_send.at[j, c], recv_sem=r_recv.at[slot, c],
            device_id={"tp": z + 1 if up else z - 1}, device_id_type=MESH,
        )

    for k in range(n - 1):
        for p in range(pieces):
            pl.when(z == 0)(lambda: r_copy(p, n - 1 - k, True, o).start())
            pl.when(z == n - 1)(lambda: r_copy(p, k, False, o).start())

    @pl.when(helper)
    def _():
        @pl.loop(0, half)
        def _(k):
            @pl.when(k != mine_k)
            def _():
                for c in range(GATHER_CHUNKS):
                    spread_came(k, c)
            to_twin(k).start()

        @pl.loop(0, half)
        def _(k):
            piece = slice_of(far, 2 * k + 1 - core, None)
            pltpu.make_async_copy(piece, piece, t_recv.at[k]).wait()

        for b in range(blocks):
            far_copy(b).start()
        for b in range(blocks):
            far_copy(b).wait()

    def landed(c, slot):
        ref = land.at[slot, c]
        pltpu.make_async_copy(ref, ref, r_recv.at[slot, c]).wait()

    def arrived(c, slot):
        landed(c, slot)
        return land[slot, c].astype(F32)

    def add_landed(c, j):
        mine = pl.ds(j * rows, rows)
        part[c, mine, :] = (part[c, mine, :].astype(F32) + arrived(c, j)).astype(BF)

    def outer_term(c, slot):
        total = jnp.zeros((rows, ow), F32)
        for p in range(pieces):
            at = pl.ds(pl.multiple_of((c // pieces) * width + p * ow, ow), ow)
            cols = pl.ds(pl.multiple_of((c % pieces) * ow, ow), ow)
            total += jnp.dot(land[slot, p], w[0, at, cols], preferred_element_type=F32)
        return total

    def add_outer(c, j):
        mine = pl.ds(j * rows, rows)
        part[c, mine, :] = (part[c, mine, :].astype(F32) + outer_term(c, j)).astype(BF)

    @pl.loop(0, outs)
    def _(c):
        cols = pl.ds(pl.multiple_of(c * ow, ow), ow)
        part[c] = jnp.dot(o[...], wo[:, cols], preferred_element_type=F32).astype(BF)

    for k in range(n - 2):
        up_j, down_j = n - 1 - k, k

        @pl.when(z == 1)
        def _():
            for p in range(pieces):
                landed(p, up_j)

        @pl.when(z == n - 2)
        def _():
            for p in range(pieces):
                landed(p, down_j)

        @pl.loop(0, outs)
        def _(c):
            @pl.when((z < up_j) & (z > 0))
            def _():
                pl.when(z > 1)(lambda: add_landed(c, up_j))
                pl.when(z == 1)(lambda: add_outer(c, up_j))
                r_copy(c, up_j, True).start()

            @pl.when((z > down_j) & (z < n - 1))
            def _():
                pl.when(z < n - 2)(lambda: add_landed(c, down_j))
                pl.when(z == n - 2)(lambda: add_outer(c, down_j))
                r_copy(c, down_j, False).start()

    @pl.when(z == 1)
    def _():
        for p in range(pieces):
            landed(p, 1)

    @pl.when(z == n - 2)
    def _():
        for p in range(pieces):
            landed(p, n)

    @pl.loop(0, outs)
    def _(c):
        cols = pl.ds(pl.multiple_of(c * ow, ow), ow)
        mine = pl.ds(pl.multiple_of(z * rows, rows), rows)
        total = part[c, mine, :].astype(F32)

        @pl.when(z == 0)
        def _():
            out_ref[:, cols] = (total + arrived(c, n)).astype(BF)

        @pl.when(z == n - 1)
        def _():
            out_ref[:, cols] = (total + arrived(c, n - 1)).astype(BF)

        @pl.when(z == 1)
        def _():
            out_ref[:, cols] = (total + outer_term(c, 1) + arrived(c, n)).astype(BF)

        @pl.when(z == n - 2)
        def _():
            out_ref[:, cols] = (total + outer_term(c, n) + arrived(c, n - 2)).astype(BF)

        if n > 4:
            @pl.when((z > 1) & (z < n - 2))
            def _():
                out_ref[:, cols] = (total + arrived(c, z) + arrived(c, n)).astype(BF)

    @pl.loop(0, outs)
    def _(c):
        for j in range(n):
            pl.when((z < j) & (z > 0))(lambda: r_copy(c, j, True).wait_send())
            pl.when((z > j) & (z < n - 1))(lambda: r_copy(c, j, False).wait_send())

    for k in range(n - 1):
        for p in range(pieces):
            pl.when(z == 0)(lambda: r_copy(p, n - 1 - k, True, o).wait_send())
            pl.when(z == n - 1)(lambda: r_copy(p, k, False, o).wait_send())

    @pl.when(helper)
    def _():
        @pl.loop(0, half)
        def _(k):
            @pl.when(k != mine_k)
            def _():
                for c in range(GATHER_CHUNKS):
                    spread(k, c).wait_send()
            to_twin(k).wait_send()


def on_device(n, seqs, codes, exponents, w_query, w_key, w_value, norm_gain, w_out):
    toks, feats = codes.shape
    depth, width = w_query.shape
    model = w_out.shape[1]
    rows = toks // n
    ow = model // OUT_CHUNKS
    steps = seqs.bit_length() - 1
    hbm = pl.BlockSpec(memory_space=pl.ANY)
    vmem = pl.BlockSpec(memory_space=pltpu.VMEM)
    dma = pltpu.SemaphoreType.DMA
    return pl.pallas_call(
        functools.partial(kernel, n, seqs),
        out_shape=(jax.ShapeDtypeStruct((rows, model), BF), jax.ShapeDtypeStruct((width, model), BF)),
        in_specs=[hbm, vmem, hbm, hbm, hbm, vmem, hbm],
        out_specs=(vmem, hbm),
        scratch_shapes=[
            pltpu.VMEM((n, toks, feats), BF),
            pltpu.VMEM((3, depth, width), BF),
            pltpu.VMEM((width, model), BF),
            pltpu.VMEM((3, toks, width), F32),
            pltpu.VMEM((toks, HD), F32),
            pltpu.VMEM((width, HD), F32),
            pltpu.VMEM((width, HD), F32),
            pltpu.VMEM((steps, width, HD), BF),
            pltpu.VMEM((steps, width, HD), BF),
            pltpu.VMEM((OUT_CHUNKS, toks, ow), BF),
            pltpu.VMEM((n + 1, OUT_CHUNKS, rows, ow), BF),
            dma(()),
            dma((3, n)),
            dma(()),
            dma((2, n, GATHER_CHUNKS)),
            dma((n, GATHER_CHUNKS)),
            dma((steps,)),
            dma((steps,)),
            dma((n, OUT_CHUNKS)),
            dma((n + 1, OUT_CHUNKS)),
            dma((GATHER_CHUNKS,)),
            dma((GATHER_CHUNKS,)),
            dma((seqs // 2, GATHER_CHUNKS)),
            dma((seqs // 2, GATHER_CHUNKS)),
            dma((seqs // 2,)),
            dma((seqs // 2,)),
            dma((model // width,)),
        ],
        compiler_params=pltpu.CompilerParams(
            collective_id=0, has_side_effects=True, vmem_limit_bytes=62 * 1024 * 1024
        ),
        cost_estimate=pl.CostEstimate(
            flops=2 * toks * width * (3 * depth + model) + 4 * toks * toks * width,
            bytes_accessed=2 * (3 * depth * width + width * model),
            transcendentals=2 * toks * width,
        ),
    )(codes, exponents.reshape(1, toks), w_query, w_key, w_value, norm_gain.reshape(1, width), w_out)[0]


def solution(mesh):
    in_specs = (
        P("seq", "tp"), P("seq"), P(None, "tp"), P(None, "tp"), P(None, "tp"), P("tp"), P("tp", None),
    )
    body = functools.partial(on_device, mesh.shape["tp"], mesh.shape["seq"])
    return jax.shard_map(
        body, mesh=mesh, in_specs=in_specs, out_specs=P(("seq", "tp"), None), check_vma=False
    )
```

```python
import functools

import jax
import jax.numpy as jnp
from jax import lax
from jax.experimental import pallas as pl
from jax.experimental.pallas import tpu as pltpu
from jax.sharding import PartitionSpec as P

HD = 128
MESH = pl.DeviceIdType.MESH
GATHER_CHUNKS = 4
OUT_CHUNKS = 8
WINDOW = 2
LAG = 3
BF = jnp.bfloat16
F32 = jnp.float32


def feature(t):
    return jnp.where(t > 0, t + 1.0, jnp.exp(jnp.minimum(t, 0.0)))


def kernel(
    n, seqs, x_ref, exp_ref, wq_ref, wk_ref, wv_ref, gain_ref, wo_ref, out_ref,
    xg, w, wo, acc, scale, tot, pre, sbuf, rbuf, part, land,
    got, exps, gate, x_sem, swap_send, swap_recv, e_send, e_recv, back_send, back_recv, w_sem, wo_sem, g_send, g_recv, s_send, s_recv, r_send, r_recv,
):
    z = lax.axis_index("tp")
    s = lax.axis_index("seq")
    toks, feats = xg.shape[1], xg.shape[2]
    width = acc.shape[2]
    heads = width // HD
    rows = toks // n
    ow = part.shape[2]
    outs = part.shape[0]
    crows = toks // GATHER_CHUNKS
    half = seqs // 2
    steps = half.bit_length() - 1
    late = s % 2 == 1
    early = s % 2 == 0
    twin = s + 1 - 2 * (s % 2)
    trades = jnp.where(s < half, s % 2, 1 - s % 2) == 1
    keeps = jnp.where(s < half, s % 2, 1 - s % 2) == 0
    mate = jnp.where(s < half, s + half - 1, s - half + 1)
    shard = jnp.where(trades, mate, s)

    def holder(u):
        first = jnp.where(u % 2 == 0, u, u + half - 1)
        second = jnp.where(u % 2 == 1, u, u - half + 1)
        return jnp.where(u < half, first, second)

    def partner(i):
        d = 1 << i
        return holder(shard + d * (1 - 2 * ((shard // d) % 2)))

    own = pltpu.make_async_copy(x_ref, xg.at[z], x_sem)
    pl.when(keeps)(lambda: own.start())
    exps[0] = jnp.broadcast_to(exp_ref[...].astype(F32), exps.shape[1:])

    def w_copy(m, b):
        src = (wq_ref, wk_ref, wv_ref)[m]
        block = pl.ds(pl.multiple_of(b * feats, feats), feats)
        return pltpu.make_async_copy(src.at[block], w.at[m, block], w_sem.at[m, b])

    def each_block(t, fn):
        if t == 0:
            fn(z)
            return
        pl.when(z - t >= 0)(lambda: fn(z - t))
        pl.when(z + t < n)(lambda: fn(z + t))

    def start_w(b):
        for m in range(3):
            w_copy(m, b).start()

    start_w(z)

    barrier = pltpu.get_barrier_semaphore()
    for i in range(steps):
        pl.semaphore_signal(barrier, inc=1, device_id={"seq": partner(i)}, device_id_type=MESH)

    pl.semaphore_signal(barrier, inc=1, device_id={"seq": twin}, device_id_type=MESH)

    @pl.when(trades)
    def _():
        pl.semaphore_signal(barrier, inc=1, device_id={"seq": mate}, device_id_type=MESH)

    @pl.when(z > 0)
    def _():
        pl.semaphore_signal(barrier, inc=1, device_id={"tp": z - 1}, device_id_type=MESH)

    @pl.when(z < n - 1)
    def _():
        pl.semaphore_signal(barrier, inc=1, device_id={"tp": z + 1}, device_id_type=MESH)

    near = jnp.where(z > 0, 1, 0) + jnp.where(z < n - 1, 1, 0)
    pl.semaphore_wait(barrier, near + steps + 1 + jnp.where(trades, 1, 0))

    def swap(c):
        at = pl.ds(c * crows, crows)
        return pltpu.make_async_remote_copy(
            src_ref=x_ref.at[at], dst_ref=xg.at[z, at], send_sem=swap_send.at[c], recv_sem=swap_recv.at[c],
            device_id={"seq": mate}, device_id_type=MESH,
        )

    e_copy = pltpu.make_async_remote_copy(
        src_ref=exps.at[0], dst_ref=exps.at[1], send_sem=e_send, recv_sem=e_recv,
        device_id={"seq": mate}, device_id_type=MESH,
    )

    @pl.when(trades)
    def _():
        for c in range(GATHER_CHUNKS):
            swap(c).start()
        e_copy.start()

    def g_copy(b, c, up):
        chunk = xg.at[b, pl.ds(c * crows, crows)]
        return pltpu.make_async_remote_copy(
            src_ref=chunk, dst_ref=chunk,
            send_sem=g_send.at[0 if up else 1, b, c], recv_sem=g_recv.at[b, c],
            device_id={"tp": z + 1 if up else z - 1}, device_id_type=MESH,
        )

    def pass_on(b, c, up):
        if up:
            pl.when(z < n - 1)(lambda: g_copy(b, c, True).start())
        else:
            pl.when(z > 0)(lambda: g_copy(b, c, False).start())

    def send_own(c):
        pass_on(z, c, True)
        pass_on(z, c, False)

    pl.when(keeps)(lambda: own.wait())
    for c in range(GATHER_CHUNKS):
        pl.when(trades)(lambda: swap(c).wait_recv())
        pl.when(early)(lambda: send_own(c))

    @pl.when(trades)
    def _():
        e_copy.wait()
        exps[0] = exps[1]
        for c in range(GATHER_CHUNKS):
            swap(c).wait_send()

    for t in range(1, n):
        each_block(t, start_w)
    wo_copy = pltpu.make_async_copy(wo_ref, wo, wo_sem)
    wo_copy.start()

    on_diagonal = lax.broadcasted_iota(jnp.int32, (toks, toks), 0) == lax.broadcasted_iota(
        jnp.int32, (toks, toks), 1
    )
    row_scale = jnp.where(on_diagonal, jnp.exp2(exps[0, 0:1, :]), 0.0)
    scale[...] = jnp.broadcast_to(jnp.sum(row_scale, axis=1, keepdims=True), scale.shape)

    tile = min(256, width)

    def project(b, m, first):
        w_copy(m, b).wait()
        block = pl.ds(pl.multiple_of(b * feats, feats), feats)

        @pl.loop(0, width // tile)
        def _(j):
            cols = pl.ds(pl.multiple_of(j * tile, tile), tile)
            term = jnp.dot(xg[b], w[m, block, cols], preferred_element_type=F32)
            if first:
                acc[m, :, cols] = term
            else:
                acc[m, :, cols] += term

    def project_all(first):
        def go(b):
            for m in (1, 2, 0):
                project(b, m, first)
        return go

    project_all(True)(z)

    @pl.when(late)
    def _():
        pl.semaphore_wait(gate, 1)
        for c in range(GATHER_CHUNKS):
            send_own(c)

    for t in range(1, n):
        for c in range(GATHER_CHUNKS):
            @pl.when(z - t >= 0)
            def _():
                g_copy(z - t, c, True).wait_recv()
                pass_on(z - t, c, True)

            @pl.when(z + t < n)
            def _():
                g_copy(z + t, c, False).wait_recv()
                pass_on(z + t, c, False)
        each_block(t, project_all(False))

    for t in range(n):
        for c in range(GATHER_CHUNKS):
            @pl.when((z - t >= 0) & (z < n - 1))
            def _():
                g_copy(z - t, c, True).wait_send()

            @pl.when((z + t < n) & (z > 0))
            def _():
                g_copy(z + t, c, False).wait_send()

    @pl.when(early)
    def _():
        pl.semaphore_signal(gate, inc=1, device_id={"seq": twin}, device_id_type=MESH)

    fk, vb, fq, o = xg.at[0], xg.at[1], xg.at[2], xg.at[3]

    def head(h):
        return pl.ds(pl.multiple_of(h * HD, HD), HD)

    @pl.loop(0, heads)
    def _(h):
        cols = head(h)
        key = feature(acc[1, :, cols] * scale[...]).astype(BF)
        val = (acc[2, :, cols] * scale[...]).astype(BF)
        fk[:, cols] = key
        vb[:, cols] = val
        tot[cols, :] = lax.dot_general(key, val, (((0,), (0,)), ((), ())), preferred_element_type=F32)

    pre[...] = jnp.zeros_like(pre)
    at_or_before = lax.broadcasted_iota(jnp.int32, (toks, toks), 0) >= lax.broadcasted_iota(
        jnp.int32, (toks, toks), 1
    )

    def intra(h):
        cols = head(h)
        qry = feature(acc[0, :, cols] * scale[...]).astype(BF)
        fq[:, cols] = qry
        scores = lax.dot_general(qry, fk[:, cols], (((1,), (1,)), ((), ())), preferred_element_type=F32)
        scores = jnp.where(at_or_before, scores, 0.0).astype(BF)
        acc[0, :, cols] = jnp.dot(scores, vb[:, cols], preferred_element_type=F32)

    def s_copy(i):
        return pltpu.make_async_remote_copy(
            src_ref=sbuf.at[i], dst_ref=rbuf.at[i], send_sem=s_send.at[i], recv_sem=s_recv.at[i],
            device_id={"seq": partner(i)}, device_id_type=MESH,
        )

    for i in range(steps):
        sbuf[i] = tot[...].astype(BF)
        s_copy(i).start()
        pl.loop(i * heads // steps, (i + 1) * heads // steps)(intra)
        s_copy(i).wait()
        came = rbuf[i].astype(F32)
        tot[...] += came

        @pl.when((shard // (1 << i)) % 2 == 1)
        def _():
            pre[...] += came

    first_half = pltpu.make_async_remote_copy(
        src_ref=sbuf.at[steps], dst_ref=rbuf.at[steps], send_sem=s_send.at[steps], recv_sem=s_recv.at[steps],
        device_id={"seq": twin}, device_id_type=MESH,
    )

    @pl.when(early)
    def _():
        sbuf[steps] = tot[...].astype(BF)
        first_half.start()

    @pl.when(late)
    def _():
        first_half.wait_recv()
        pre[...] += rbuf[steps].astype(F32)

    @pl.loop(0, heads)
    def _(h):
        cols = head(h)
        y = acc[0, :, cols] + jnp.dot(fq[:, cols], pre[cols, :].astype(BF), preferred_element_type=F32)
        mean_sq = jnp.mean(y * y, axis=-1, keepdims=True)
        o[:, cols] = (y * lax.rsqrt(mean_sq + 1e-05) * gain_ref[:, cols]).astype(BF)

    wo_copy.wait()

    def r_copy(c, j, up):
        src = part.at[c, pl.ds(j * rows, rows)]
        slot = j if up else jnp.where(z - 1 == j, n, j)
        return pltpu.make_async_remote_copy(
            src_ref=src, dst_ref=land.at[slot, c],
            send_sem=r_send.at[j, c], recv_sem=r_recv.at[slot, c],
            device_id={"tp": z + 1 if up else z - 1}, device_id_type=MESH,
        )

    def landed(c, slot):
        ref = land.at[slot, c]
        pltpu.make_async_copy(ref, ref, r_recv.at[slot, c]).wait()

    def arrived(c, slot):
        landed(c, slot)
        return land[slot, c].astype(F32)

    def add_landed(c, j):
        mine = pl.ds(j * rows, rows)
        part[c, mine, :] = (part[c, mine, :].astype(F32) + arrived(c, j)).astype(BF)

    def back(c):
        mine = pl.ds(pl.multiple_of(z * rows, rows), rows)
        return pltpu.make_async_remote_copy(
            src_ref=part.at[c, mine], dst_ref=got.at[c], send_sem=back_send.at[c], recv_sem=back_recv.at[c],
            device_id={"seq": mate}, device_id_type=MESH,
        )

    def finish(c):
        cols = pl.ds(pl.multiple_of(c * ow, ow), ow)
        mine = pl.ds(pl.multiple_of(z * rows, rows), rows)
        pl.when(z > 0)(lambda: landed(c, z))
        pl.when(z < n - 1)(lambda: landed(c, n))

        def give(total):
            @pl.when(keeps)
            def _():
                out_ref[:, cols] = total.astype(BF)

            @pl.when(trades)
            def _():
                part[c, mine, :] = total.astype(BF)

        total = part[c, mine, :].astype(F32)
        pl.when(z == 0)(lambda: give(total + land[n, c].astype(F32)))
        pl.when(z == n - 1)(lambda: give(total + land[n - 1, c].astype(F32)))
        pl.when((z > 0) & (z < n - 1))(
            lambda: give(total + land[z, c].astype(F32) + land[n, c].astype(F32))
        )
        pl.when(trades)(lambda: back(c).start())

    def sent(c):
        for j in range(n):
            pl.when(z < j)(lambda: r_copy(c, j, True).wait_send())
            pl.when(z > j)(lambda: r_copy(c, j, False).wait_send())

    @pl.loop(0, outs)
    def _(c):
        cols = pl.ds(pl.multiple_of(c * ow, ow), ow)
        part[c] = jnp.dot(o[...], wo[:, cols], preferred_element_type=F32).astype(BF)
        pl.when(c >= WINDOW)(lambda: sent(c - WINDOW))
        for k in range(n - 1):
            up_j, down_j = n - 1 - k, k

            @pl.when(z < up_j)
            def _():
                pl.when(z > 0)(lambda: add_landed(c, up_j))
                r_copy(c, up_j, True).start()

            @pl.when(z > down_j)
            def _():
                pl.when(z < n - 1)(lambda: add_landed(c, down_j))
                r_copy(c, down_j, False).start()
        pl.when(c >= LAG)(lambda: finish(c - LAG))

    pl.loop(outs - LAG, outs)(finish)
    pl.loop(outs - WINDOW, outs)(sent)

    @pl.when(trades)
    def _():
        @pl.loop(0, outs)
        def _(c):
            back(c).wait()
            out_ref[:, pl.ds(pl.multiple_of(c * ow, ow), ow)] = got[c]

    pl.when(early)(lambda: first_half.wait_send())


def on_device(n, seqs, codes, exponents, w_query, w_key, w_value, norm_gain, w_out):
    toks, feats = codes.shape
    depth, width = w_query.shape
    model = w_out.shape[1]
    rows = toks // n
    ow = model // OUT_CHUNKS
    steps = (seqs // 2).bit_length() - 1
    hbm = pl.BlockSpec(memory_space=pl.ANY)
    vmem = pl.BlockSpec(memory_space=pltpu.VMEM)
    dma = pltpu.SemaphoreType.DMA
    return pl.pallas_call(
        functools.partial(kernel, n, seqs),
        out_shape=jax.ShapeDtypeStruct((rows, model), BF),
        in_specs=[hbm, vmem, hbm, hbm, hbm, vmem, hbm],
        out_specs=vmem,
        scratch_shapes=[
            pltpu.VMEM((n, toks, feats), BF),
            pltpu.VMEM((3, depth, width), BF),
            pltpu.VMEM((width, model), BF),
            pltpu.VMEM((3, toks, width), F32),
            pltpu.VMEM((toks, HD), F32),
            pltpu.VMEM((width, HD), F32),
            pltpu.VMEM((width, HD), F32),
            pltpu.VMEM((steps + 1, width, HD), BF),
            pltpu.VMEM((steps + 1, width, HD), BF),
            pltpu.VMEM((OUT_CHUNKS, toks, ow), BF),
            pltpu.VMEM((n + 1, OUT_CHUNKS, rows, ow), BF),
            pltpu.VMEM((OUT_CHUNKS, rows, ow), BF),
            pltpu.VMEM((2, 8, toks), F32),
            pltpu.SemaphoreType.REGULAR,
            dma(()),
            dma((GATHER_CHUNKS,)),
            dma((GATHER_CHUNKS,)),
            dma(()),
            dma(()),
            dma((OUT_CHUNKS,)),
            dma((OUT_CHUNKS,)),
            dma((3, n)),
            dma(()),
            dma((2, n, GATHER_CHUNKS)),
            dma((n, GATHER_CHUNKS)),
            dma((steps + 1,)),
            dma((steps + 1,)),
            dma((n, OUT_CHUNKS)),
            dma((n + 1, OUT_CHUNKS)),
        ],
        compiler_params=pltpu.CompilerParams(
            collective_id=0, has_side_effects=True, vmem_limit_bytes=62 * 1024 * 1024
        ),
        cost_estimate=pl.CostEstimate(
            flops=2 * toks * width * (3 * depth + model) + 4 * toks * toks * width,
            bytes_accessed=2 * (3 * depth * width + width * model),
            transcendentals=2 * toks * width,
        ),
    )(codes, exponents.reshape(1, toks), w_query, w_key, w_value, norm_gain.reshape(1, width), w_out)


def solution(mesh):
    in_specs = (
        P("seq", "tp"), P("seq"), P(None, "tp"), P(None, "tp"), P(None, "tp"), P("tp"), P("tp", None),
    )
    body = functools.partial(on_device, mesh.shape["tp"], mesh.shape["seq"])
    return jax.shard_map(
        body, mesh=mesh, in_specs=in_specs, out_specs=P(("seq", "tp"), None), check_vma=False
    )
```

```python
import functools

import jax
import jax.numpy as jnp
from jax import lax
from jax.experimental import pallas as pl
from jax.experimental.pallas import tpu as pltpu
from jax.sharding import PartitionSpec as P

HD = 128
MESH = pl.DeviceIdType.MESH
GATHER_CHUNKS = 4
OUT_CHUNKS = 8
WINDOW = 4
LAG = 3
BF = jnp.bfloat16
F32 = jnp.float32


def feature(t):
    return jnp.where(t > 0, t + 1.0, jnp.exp(jnp.minimum(t, 0.0)))


def kernel(
    n, seqs, x_ref, exp_ref, wq_ref, wk_ref, wv_ref, gain_ref, wo_ref, out_ref,
    xg, w, wo, acc, scale, tot, pre, sbuf, rbuf, part, land,
    got, exps, gate, x_sem, swap_send, swap_recv, e_send, e_recv, back_send, back_recv, w_sem, wo_sem, g_send, g_recv, s_send, s_recv, r_send, r_recv,
):
    z = lax.axis_index("tp")
    s = lax.axis_index("seq")
    toks, feats = xg.shape[1], xg.shape[2]
    width = acc.shape[2]
    heads = width // HD
    rows = toks // n
    ow = part.shape[2]
    outs = part.shape[0]
    crows = toks // GATHER_CHUNKS
    half = seqs // 2
    steps = half.bit_length() - 1
    late = s % 2 == 1
    early = s % 2 == 0
    twin = s + 1 - 2 * (s % 2)
    trades = jnp.where(s < half, s % 2, 1 - s % 2) == 1
    keeps = jnp.where(s < half, s % 2, 1 - s % 2) == 0
    mate = jnp.where(s < half, s + half - 1, s - half + 1)
    shard = jnp.where(trades, mate, s)

    def holder(u):
        first = jnp.where(u % 2 == 0, u, u + half - 1)
        second = jnp.where(u % 2 == 1, u, u - half + 1)
        return jnp.where(u < half, first, second)

    def partner(i):
        d = 1 << i
        return holder(shard + d * (1 - 2 * ((shard // d) % 2)))

    own = pltpu.make_async_copy(x_ref, xg.at[z], x_sem)
    pl.when(keeps)(lambda: own.start())
    exps[0] = jnp.broadcast_to(exp_ref[...].astype(F32), exps.shape[1:])

    def w_copy(m, b):
        src = (wq_ref, wk_ref, wv_ref)[m]
        block = pl.ds(pl.multiple_of(b * feats, feats), feats)
        return pltpu.make_async_copy(src.at[block], w.at[m, block], w_sem.at[m, b])

    def each_block(t, fn):
        if t == 0:
            fn(z)
            return
        pl.when(z - t >= 0)(lambda: fn(z - t))
        pl.when(z + t < n)(lambda: fn(z + t))

    def start_w(b):
        for m in range(3):
            w_copy(m, b).start()

    start_w(z)

    barrier = pltpu.get_barrier_semaphore()
    for i in range(steps):
        pl.semaphore_signal(barrier, inc=1, device_id={"seq": partner(i)}, device_id_type=MESH)

    pl.semaphore_signal(barrier, inc=1, device_id={"seq": twin}, device_id_type=MESH)

    @pl.when(trades)
    def _():
        pl.semaphore_signal(barrier, inc=1, device_id={"seq": mate}, device_id_type=MESH)

    @pl.when(z > 0)
    def _():
        pl.semaphore_signal(barrier, inc=1, device_id={"tp": z - 1}, device_id_type=MESH)

    @pl.when(z < n - 1)
    def _():
        pl.semaphore_signal(barrier, inc=1, device_id={"tp": z + 1}, device_id_type=MESH)

    near = jnp.where(z > 0, 1, 0) + jnp.where(z < n - 1, 1, 0)
    pl.semaphore_wait(barrier, near + steps + 1 + jnp.where(trades, 1, 0))

    def swap(c):
        at = pl.ds(c * crows, crows)
        return pltpu.make_async_remote_copy(
            src_ref=x_ref.at[at], dst_ref=xg.at[z, at], send_sem=swap_send.at[c], recv_sem=swap_recv.at[c],
            device_id={"seq": mate}, device_id_type=MESH,
        )

    e_copy = pltpu.make_async_remote_copy(
        src_ref=exps.at[0], dst_ref=exps.at[1], send_sem=e_send, recv_sem=e_recv,
        device_id={"seq": mate}, device_id_type=MESH,
    )

    @pl.when(trades)
    def _():
        for c in range(GATHER_CHUNKS):
            swap(c).start()
        e_copy.start()

    def g_copy(b, c, up):
        chunk = xg.at[b, pl.ds(c * crows, crows)]
        return pltpu.make_async_remote_copy(
            src_ref=chunk, dst_ref=chunk,
            send_sem=g_send.at[0 if up else 1, b, c], recv_sem=g_recv.at[b, c],
            device_id={"tp": z + 1 if up else z - 1}, device_id_type=MESH,
        )

    def pass_on(b, c, up):
        if up:
            pl.when(z < n - 1)(lambda: g_copy(b, c, True).start())
        else:
            pl.when(z > 0)(lambda: g_copy(b, c, False).start())

    def send_own(c):
        pass_on(z, c, True)
        pass_on(z, c, False)

    pl.when(keeps)(lambda: own.wait())
    for c in range(GATHER_CHUNKS):
        pl.when(trades)(lambda: swap(c).wait_recv())
        pl.when(early)(lambda: send_own(c))

    @pl.when(trades)
    def _():
        e_copy.wait()
        exps[0] = exps[1]
        for c in range(GATHER_CHUNKS):
            swap(c).wait_send()

    for t in range(1, n):
        each_block(t, start_w)
    wo_copy = pltpu.make_async_copy(wo_ref, wo, wo_sem)
    wo_copy.start()

    on_diagonal = lax.broadcasted_iota(jnp.int32, (toks, toks), 0) == lax.broadcasted_iota(
        jnp.int32, (toks, toks), 1
    )
    row_scale = jnp.where(on_diagonal, jnp.exp2(exps[0, 0:1, :]), 0.0)
    scale[...] = jnp.broadcast_to(jnp.sum(row_scale, axis=1, keepdims=True), scale.shape)

    tile = min(512, width)

    def project(b, m, first):
        w_copy(m, b).wait()
        block = pl.ds(pl.multiple_of(b * feats, feats), feats)

        @pl.loop(0, width // tile)
        def _(j):
            cols = pl.ds(pl.multiple_of(j * tile, tile), tile)
            term = jnp.dot(xg[b], w[m, block, cols], preferred_element_type=F32)
            if first:
                acc[m, :, cols] = term
            else:
                acc[m, :, cols] += term

    def project_all(first):
        def go(b):
            for m in (1, 2, 0):
                project(b, m, first)
        return go

    project_all(True)(z)

    @pl.when(late)
    def _():
        pl.semaphore_wait(gate, 1)
        for c in range(GATHER_CHUNKS):
            send_own(c)

    for t in range(1, n):
        for c in range(GATHER_CHUNKS):
            @pl.when(z - t >= 0)
            def _():
                g_copy(z - t, c, True).wait_recv()
                pass_on(z - t, c, True)

            @pl.when(z + t < n)
            def _():
                g_copy(z + t, c, False).wait_recv()
                pass_on(z + t, c, False)
        if t == max(n - 2, 1):
            @pl.when(early)
            def _():
                pl.semaphore_signal(gate, inc=1, device_id={"seq": twin}, device_id_type=MESH)

        each_block(t, project_all(False))

    for t in range(n):
        for c in range(GATHER_CHUNKS):
            @pl.when((z - t >= 0) & (z < n - 1))
            def _():
                g_copy(z - t, c, True).wait_send()

            @pl.when((z + t < n) & (z > 0))
            def _():
                g_copy(z + t, c, False).wait_send()

    fk, vb, fq, o = xg.at[0], xg.at[1], xg.at[2], xg.at[3]

    def head(h):
        return pl.ds(pl.multiple_of(h * HD, HD), HD)

    @pl.loop(0, heads)
    def _(h):
        cols = head(h)
        key = feature(acc[1, :, cols] * scale[...]).astype(BF)
        val = (acc[2, :, cols] * scale[...]).astype(BF)
        fk[:, cols] = key
        vb[:, cols] = val
        tot[cols, :] = lax.dot_general(key, val, (((0,), (0,)), ((), ())), preferred_element_type=F32)

    pre[...] = jnp.zeros_like(pre)
    at_or_before = lax.broadcasted_iota(jnp.int32, (toks, toks), 0) >= lax.broadcasted_iota(
        jnp.int32, (toks, toks), 1
    )

    def intra(h):
        cols = head(h)
        qry = feature(acc[0, :, cols] * scale[...]).astype(BF)
        fq[:, cols] = qry
        scores = lax.dot_general(qry, fk[:, cols], (((1,), (1,)), ((), ())), preferred_element_type=F32)
        scores = jnp.where(at_or_before, scores, 0.0).astype(BF)
        acc[0, :, cols] = jnp.dot(scores, vb[:, cols], preferred_element_type=F32)

    def s_copy(i):
        return pltpu.make_async_remote_copy(
            src_ref=sbuf.at[i], dst_ref=rbuf.at[i], send_sem=s_send.at[i], recv_sem=s_recv.at[i],
            device_id={"seq": partner(i)}, device_id_type=MESH,
        )

    for i in range(steps):
        sbuf[i] = tot[...].astype(BF)
        s_copy(i).start()
        pl.loop(i * heads // steps, (i + 1) * heads // steps)(intra)
        s_copy(i).wait()
        came = rbuf[i].astype(F32)
        tot[...] += came

        @pl.when((shard // (1 << i)) % 2 == 1)
        def _():
            pre[...] += came

    first_half = pltpu.make_async_remote_copy(
        src_ref=sbuf.at[steps], dst_ref=rbuf.at[steps], send_sem=s_send.at[steps], recv_sem=s_recv.at[steps],
        device_id={"seq": twin}, device_id_type=MESH,
    )

    @pl.when(early)
    def _():
        sbuf[steps] = tot[...].astype(BF)
        first_half.start()

    @pl.when(late)
    def _():
        first_half.wait_recv()
        pre[...] += rbuf[steps].astype(F32)

    @pl.loop(0, heads)
    def _(h):
        cols = head(h)
        y = acc[0, :, cols] + jnp.dot(fq[:, cols], pre[cols, :].astype(BF), preferred_element_type=F32)
        mean_sq = jnp.mean(y * y, axis=-1, keepdims=True)
        o[:, cols] = (y * lax.rsqrt(mean_sq + 1e-05) * gain_ref[:, cols]).astype(BF)

    wo_copy.wait()

    def r_copy(c, j, up):
        src = part.at[c, pl.ds(j * rows, rows)]
        slot = j if up else jnp.where(z - 1 == j, n, j)
        return pltpu.make_async_remote_copy(
            src_ref=src, dst_ref=land.at[slot, c],
            send_sem=r_send.at[j, c], recv_sem=r_recv.at[slot, c],
            device_id={"tp": z + 1 if up else z - 1}, device_id_type=MESH,
        )

    def landed(c, slot):
        ref = land.at[slot, c]
        pltpu.make_async_copy(ref, ref, r_recv.at[slot, c]).wait()

    def arrived(c, slot):
        landed(c, slot)
        return land[slot, c].astype(F32)

    def add_landed(c, j):
        mine = pl.ds(j * rows, rows)
        part[c, mine, :] = (part[c, mine, :].astype(F32) + arrived(c, j)).astype(BF)

    def back(c):
        mine = pl.ds(pl.multiple_of(z * rows, rows), rows)
        return pltpu.make_async_remote_copy(
            src_ref=part.at[c, mine], dst_ref=got.at[c], send_sem=back_send.at[c], recv_sem=back_recv.at[c],
            device_id={"seq": mate}, device_id_type=MESH,
        )

    def finish(c):
        cols = pl.ds(pl.multiple_of(c * ow, ow), ow)
        mine = pl.ds(pl.multiple_of(z * rows, rows), rows)
        pl.when(z > 0)(lambda: landed(c, z))
        pl.when(z < n - 1)(lambda: landed(c, n))

        def give(total):
            @pl.when(keeps)
            def _():
                out_ref[:, cols] = total.astype(BF)

            @pl.when(trades)
            def _():
                part[c, mine, :] = total.astype(BF)

        total = part[c, mine, :].astype(F32)
        pl.when(z == 0)(lambda: give(total + land[n, c].astype(F32)))
        pl.when(z == n - 1)(lambda: give(total + land[n - 1, c].astype(F32)))
        pl.when((z > 0) & (z < n - 1))(
            lambda: give(total + land[z, c].astype(F32) + land[n, c].astype(F32))
        )
        pl.when(trades)(lambda: back(c).start())

    def sent(c):
        for j in range(n):
            pl.when(z < j)(lambda: r_copy(c, j, True).wait_send())
            pl.when(z > j)(lambda: r_copy(c, j, False).wait_send())

    @pl.loop(0, outs)
    def _(c):
        cols = pl.ds(pl.multiple_of(c * ow, ow), ow)
        part[c] = jnp.dot(o[...], wo[:, cols], preferred_element_type=F32).astype(BF)
        pl.when(c >= WINDOW)(lambda: sent(c - WINDOW))
        for k in range(n - 1):
            up_j, down_j = n - 1 - k, k

            @pl.when(z < up_j)
            def _():
                pl.when(z > 0)(lambda: add_landed(c, up_j))
                r_copy(c, up_j, True).start()

            @pl.when(z > down_j)
            def _():
                pl.when(z < n - 1)(lambda: add_landed(c, down_j))
                r_copy(c, down_j, False).start()
        pl.when(c >= LAG)(lambda: finish(c - LAG))

    pl.loop(outs - LAG, outs)(finish)
    pl.loop(outs - WINDOW, outs)(sent)

    @pl.when(trades)
    def _():
        @pl.loop(0, outs)
        def _(c):
            back(c).wait()
            out_ref[:, pl.ds(pl.multiple_of(c * ow, ow), ow)] = got[c]

    pl.when(early)(lambda: first_half.wait_send())


def on_device(n, seqs, codes, exponents, w_query, w_key, w_value, norm_gain, w_out):
    toks, feats = codes.shape
    depth, width = w_query.shape
    model = w_out.shape[1]
    rows = toks // n
    ow = model // OUT_CHUNKS
    steps = (seqs // 2).bit_length() - 1
    hbm = pl.BlockSpec(memory_space=pl.ANY)
    vmem = pl.BlockSpec(memory_space=pltpu.VMEM)
    dma = pltpu.SemaphoreType.DMA
    return pl.pallas_call(
        functools.partial(kernel, n, seqs),
        out_shape=jax.ShapeDtypeStruct((rows, model), BF),
        in_specs=[hbm, vmem, hbm, hbm, hbm, vmem, hbm],
        out_specs=vmem,
        scratch_shapes=[
            pltpu.VMEM((n, toks, feats), BF),
            pltpu.VMEM((3, depth, width), BF),
            pltpu.VMEM((width, model), BF),
            pltpu.VMEM((3, toks, width), F32),
            pltpu.VMEM((toks, HD), F32),
            pltpu.VMEM((width, HD), F32),
            pltpu.VMEM((width, HD), F32),
            pltpu.VMEM((steps + 1, width, HD), BF),
            pltpu.VMEM((steps + 1, width, HD), BF),
            pltpu.VMEM((OUT_CHUNKS, toks, ow), BF),
            pltpu.VMEM((n + 1, OUT_CHUNKS, rows, ow), BF),
            pltpu.VMEM((OUT_CHUNKS, rows, ow), BF),
            pltpu.VMEM((2, 8, toks), F32),
            pltpu.SemaphoreType.REGULAR,
            dma(()),
            dma((GATHER_CHUNKS,)),
            dma((GATHER_CHUNKS,)),
            dma(()),
            dma(()),
            dma((OUT_CHUNKS,)),
            dma((OUT_CHUNKS,)),
            dma((3, n)),
            dma(()),
            dma((2, n, GATHER_CHUNKS)),
            dma((n, GATHER_CHUNKS)),
            dma((steps + 1,)),
            dma((steps + 1,)),
            dma((n, OUT_CHUNKS)),
            dma((n + 1, OUT_CHUNKS)),
        ],
        compiler_params=pltpu.CompilerParams(
            collective_id=0, has_side_effects=True, vmem_limit_bytes=62 * 1024 * 1024
        ),
        cost_estimate=pl.CostEstimate(
            flops=2 * toks * width * (3 * depth + model) + 4 * toks * toks * width,
            bytes_accessed=2 * (3 * depth * width + width * model),
            transcendentals=2 * toks * width,
        ),
    )(codes, exponents.reshape(1, toks), w_query, w_key, w_value, norm_gain.reshape(1, width), w_out)


def solution(mesh):
    in_specs = (
        P("seq", "tp"), P("seq"), P(None, "tp"), P(None, "tp"), P(None, "tp"), P("tp"), P("tp", None),
    )
    body = functools.partial(on_device, mesh.shape["tp"], mesh.shape["seq"])
    return jax.shard_map(
        body, mesh=mesh, in_specs=in_specs, out_specs=P(("seq", "tp"), None), check_vma=False
    )
```

```python
import functools

import jax
import jax.numpy as jnp
from jax import lax
from jax.experimental import pallas as pl
from jax.experimental.pallas import tpu as pltpu
from jax.sharding import PartitionSpec as P

HD = 128
MESH = pl.DeviceIdType.MESH
GATHER_CHUNKS = 4
OUT_CHUNKS = 8
WINDOW = 4
LAG = 3
BF = jnp.bfloat16
F32 = jnp.float32


def feature(t):
    return jnp.where(t > 0, t + 1.0, jnp.exp(jnp.minimum(t, 0.0)))


def kernel(
    n, seqs, x_ref, exp_ref, wq_ref, wk_ref, wv_ref, gain_ref, wo_ref, out_ref,
    xg, w, wo, acc, scale, tot, pre, sbuf, rbuf, part, land,
    got, exps, gate, x_sem, swap_send, swap_recv, e_send, e_recv, back_send, back_recv, w_sem, wo_sem, g_send, g_recv, s_send, s_recv, r_send, r_recv,
):
    z = lax.axis_index("tp")
    s = lax.axis_index("seq")
    toks, feats = xg.shape[1], xg.shape[2]
    width = acc.shape[2]
    heads = width // HD
    rows = toks // n
    ow = part.shape[2]
    outs = part.shape[0]
    crows = toks // GATHER_CHUNKS
    half = seqs // 2
    steps = half.bit_length() - 1
    late = s % 2 == 1
    early = s % 2 == 0
    twin = s + 1 - 2 * (s % 2)
    trades = jnp.where(s < half, s % 2, 1 - s % 2) == 1
    keeps = jnp.where(s < half, s % 2, 1 - s % 2) == 0
    mate = jnp.where(s < half, s + half - 1, s - half + 1)
    shard = jnp.where(trades, mate, s)

    def holder(u):
        first = jnp.where(u % 2 == 0, u, u + half - 1)
        second = jnp.where(u % 2 == 1, u, u - half + 1)
        return jnp.where(u < half, first, second)

    def partner(i):
        d = 1 << i
        return holder(shard + d * (1 - 2 * ((shard // d) % 2)))

    own = pltpu.make_async_copy(x_ref, xg.at[z], x_sem)
    pl.when(keeps)(lambda: own.start())
    exps[0] = jnp.broadcast_to(exp_ref[...].astype(F32), exps.shape[1:])

    def w_copy(m, b):
        src = (wq_ref, wk_ref, wv_ref)[m]
        block = pl.ds(pl.multiple_of(b * feats, feats), feats)
        return pltpu.make_async_copy(src.at[block], w.at[m, block], w_sem.at[m, b])

    def each_block(t, fn):
        if t == 0:
            fn(z)
            return
        pl.when(z - t >= 0)(lambda: fn(z - t))
        pl.when(z + t < n)(lambda: fn(z + t))

    def start_w(b):
        for m in range(3):
            w_copy(m, b).start()

    start_w(z)

    barrier = pltpu.get_barrier_semaphore()
    for i in range(steps):
        pl.semaphore_signal(barrier, inc=1, device_id={"seq": partner(i)}, device_id_type=MESH)

    pl.semaphore_signal(barrier, inc=1, device_id={"seq": twin}, device_id_type=MESH)

    @pl.when(trades)
    def _():
        pl.semaphore_signal(barrier, inc=1, device_id={"seq": mate}, device_id_type=MESH)

    @pl.when(z > 0)
    def _():
        pl.semaphore_signal(barrier, inc=1, device_id={"tp": z - 1}, device_id_type=MESH)

    @pl.when(z < n - 1)
    def _():
        pl.semaphore_signal(barrier, inc=1, device_id={"tp": z + 1}, device_id_type=MESH)

    near = jnp.where(z > 0, 1, 0) + jnp.where(z < n - 1, 1, 0)
    pl.semaphore_wait(barrier, near + steps + 1 + jnp.where(trades, 1, 0))

    def swap(c):
        at = pl.ds(c * crows, crows)
        return pltpu.make_async_remote_copy(
            src_ref=x_ref.at[at], dst_ref=xg.at[z, at], send_sem=swap_send.at[c], recv_sem=swap_recv.at[c],
            device_id={"seq": mate}, device_id_type=MESH,
        )

    e_copy = pltpu.make_async_remote_copy(
        src_ref=exps.at[0], dst_ref=exps.at[1], send_sem=e_send, recv_sem=e_recv,
        device_id={"seq": mate}, device_id_type=MESH,
    )

    @pl.when(trades)
    def _():
        for c in range(GATHER_CHUNKS):
            swap(c).start()
        e_copy.start()

    def g_copy(b, c, up):
        chunk = xg.at[b, pl.ds(c * crows, crows)]
        return pltpu.make_async_remote_copy(
            src_ref=chunk, dst_ref=chunk,
            send_sem=g_send.at[0 if up else 1, b, c], recv_sem=g_recv.at[b, c],
            device_id={"tp": z + 1 if up else z - 1}, device_id_type=MESH,
        )

    def pass_on(b, c, up):
        if up:
            pl.when(z < n - 1)(lambda: g_copy(b, c, True).start())
        else:
            pl.when(z > 0)(lambda: g_copy(b, c, False).start())

    def send_own(c):
        pass_on(z, c, True)
        pass_on(z, c, False)

    pl.when(keeps)(lambda: own.wait())
    for c in range(GATHER_CHUNKS):
        pl.when(trades)(lambda: swap(c).wait_recv())
        pl.when(early)(lambda: send_own(c))

    @pl.when(trades)
    def _():
        e_copy.wait()
        exps[0] = exps[1]
        for c in range(GATHER_CHUNKS):
            swap(c).wait_send()

    for t in range(1, n):
        each_block(t, start_w)
    wo_copy = pltpu.make_async_copy(wo_ref, wo, wo_sem)
    wo_copy.start()

    on_diagonal = lax.broadcasted_iota(jnp.int32, (toks, toks), 0) == lax.broadcasted_iota(
        jnp.int32, (toks, toks), 1
    )
    row_scale = jnp.where(on_diagonal, jnp.exp2(exps[0, 0:1, :]), 0.0)
    scale[...] = jnp.broadcast_to(jnp.sum(row_scale, axis=1, keepdims=True), scale.shape)

    tile = min(512, width)

    def project(b, m, first):
        w_copy(m, b).wait()
        block = pl.ds(pl.multiple_of(b * feats, feats), feats)

        @pl.loop(0, width // tile)
        def _(j):
            cols = pl.ds(pl.multiple_of(j * tile, tile), tile)
            term = jnp.dot(xg[b], w[m, block, cols], preferred_element_type=F32)
            if first:
                acc[m, :, cols] = term
            else:
                acc[m, :, cols] += term

    def project_all(first):
        def go(b):
            for m in (1, 2, 0):
                project(b, m, first)
        return go

    project_all(True)(z)

    @pl.when(late)
    def _():
        pl.semaphore_wait(gate, 1)
        for c in range(GATHER_CHUNKS):
            send_own(c)

    for t in range(1, n):
        for c in range(GATHER_CHUNKS):
            @pl.when(z - t >= 0)
            def _():
                g_copy(z - t, c, True).wait_recv()
                pass_on(z - t, c, True)

            @pl.when(z + t < n)
            def _():
                g_copy(z + t, c, False).wait_recv()
                pass_on(z + t, c, False)
        if t == 1:
            @pl.when(early)
            def _():
                pl.semaphore_signal(gate, inc=1, device_id={"seq": twin}, device_id_type=MESH)

        each_block(t, project_all(False))

    for t in range(n):
        for c in range(GATHER_CHUNKS):
            @pl.when((z - t >= 0) & (z < n - 1))
            def _():
                g_copy(z - t, c, True).wait_send()

            @pl.when((z + t < n) & (z > 0))
            def _():
                g_copy(z + t, c, False).wait_send()

    fk, vb, fq, o = xg.at[0], xg.at[1], xg.at[2], xg.at[3]

    def head(h):
        return pl.ds(pl.multiple_of(h * HD, HD), HD)

    @pl.loop(0, heads)
    def _(h):
        cols = head(h)
        key = feature(acc[1, :, cols] * scale[...]).astype(BF)
        val = (acc[2, :, cols] * scale[...]).astype(BF)
        fk[:, cols] = key
        vb[:, cols] = val
        tot[cols, :] = lax.dot_general(key, val, (((0,), (0,)), ((), ())), preferred_element_type=F32)

    pre[...] = jnp.zeros_like(pre)
    at_or_before = lax.broadcasted_iota(jnp.int32, (toks, toks), 0) >= lax.broadcasted_iota(
        jnp.int32, (toks, toks), 1
    )

    def intra(h):
        cols = head(h)
        qry = feature(acc[0, :, cols] * scale[...]).astype(BF)
        fq[:, cols] = qry
        scores = lax.dot_general(qry, fk[:, cols], (((1,), (1,)), ((), ())), preferred_element_type=F32)
        scores = jnp.where(at_or_before, scores, 0.0).astype(BF)
        acc[0, :, cols] = jnp.dot(scores, vb[:, cols], preferred_element_type=F32)

    def s_copy(i):
        return pltpu.make_async_remote_copy(
            src_ref=sbuf.at[i], dst_ref=rbuf.at[i], send_sem=s_send.at[i], recv_sem=s_recv.at[i],
            device_id={"seq": partner(i)}, device_id_type=MESH,
        )

    for i in range(steps):
        sbuf[i] = tot[...].astype(BF)
        s_copy(i).start()
        pl.loop(i * heads // steps, (i + 1) * heads // steps)(intra)
        s_copy(i).wait()
        came = rbuf[i].astype(F32)
        tot[...] += came

        @pl.when((shard // (1 << i)) % 2 == 1)
        def _():
            pre[...] += came

    first_half = pltpu.make_async_remote_copy(
        src_ref=sbuf.at[steps], dst_ref=rbuf.at[steps], send_sem=s_send.at[steps], recv_sem=s_recv.at[steps],
        device_id={"seq": twin}, device_id_type=MESH,
    )

    @pl.when(early)
    def _():
        sbuf[steps] = tot[...].astype(BF)
        first_half.start()

    @pl.when(late)
    def _():
        first_half.wait_recv()
        pre[...] += rbuf[steps].astype(F32)

    @pl.loop(0, heads)
    def _(h):
        cols = head(h)
        y = acc[0, :, cols] + jnp.dot(fq[:, cols], pre[cols, :].astype(BF), preferred_element_type=F32)
        mean_sq = jnp.mean(y * y, axis=-1, keepdims=True)
        o[:, cols] = (y * lax.rsqrt(mean_sq + 1e-05) * gain_ref[:, cols]).astype(BF)

    wo_copy.wait()

    def r_copy(c, j, up):
        src = part.at[c, pl.ds(j * rows, rows)]
        slot = j if up else jnp.where(z - 1 == j, n, j)
        return pltpu.make_async_remote_copy(
            src_ref=src, dst_ref=land.at[slot, c],
            send_sem=r_send.at[j, c], recv_sem=r_recv.at[slot, c],
            device_id={"tp": z + 1 if up else z - 1}, device_id_type=MESH,
        )

    def landed(c, slot):
        ref = land.at[slot, c]
        pltpu.make_async_copy(ref, ref, r_recv.at[slot, c]).wait()

    def arrived(c, slot):
        landed(c, slot)
        return land[slot, c].astype(F32)

    def add_landed(c, j):
        mine = pl.ds(j * rows, rows)
        part[c, mine, :] = (part[c, mine, :].astype(F32) + arrived(c, j)).astype(BF)

    def back(c):
        mine = pl.ds(pl.multiple_of(z * rows, rows), rows)
        return pltpu.make_async_remote_copy(
            src_ref=part.at[c, mine], dst_ref=got.at[c], send_sem=back_send.at[c], recv_sem=back_recv.at[c],
            device_id={"seq": mate}, device_id_type=MESH,
        )

    def finish(c):
        cols = pl.ds(pl.multiple_of(c * ow, ow), ow)
        mine = pl.ds(pl.multiple_of(z * rows, rows), rows)
        pl.when(z > 0)(lambda: landed(c, z))
        pl.when(z < n - 1)(lambda: landed(c, n))

        def give(total):
            @pl.when(keeps)
            def _():
                out_ref[:, cols] = total.astype(BF)

            @pl.when(trades)
            def _():
                part[c, mine, :] = total.astype(BF)

        total = part[c, mine, :].astype(F32)
        pl.when(z == 0)(lambda: give(total + land[n, c].astype(F32)))
        pl.when(z == n - 1)(lambda: give(total + land[n - 1, c].astype(F32)))
        pl.when((z > 0) & (z < n - 1))(
            lambda: give(total + land[z, c].astype(F32) + land[n, c].astype(F32))
        )
        pl.when(trades)(lambda: back(c).start())

    def sent(c):
        for j in range(n):
            pl.when(z < j)(lambda: r_copy(c, j, True).wait_send())
            pl.when(z > j)(lambda: r_copy(c, j, False).wait_send())

    @pl.loop(0, outs)
    def _(c):
        cols = pl.ds(pl.multiple_of(c * ow, ow), ow)
        part[c] = jnp.dot(o[...], wo[:, cols], preferred_element_type=F32).astype(BF)
        pl.when(c >= WINDOW)(lambda: sent(c - WINDOW))
        for k in range(n - 1):
            up_j, down_j = n - 1 - k, k

            @pl.when(z < up_j)
            def _():
                pl.when(z > 0)(lambda: add_landed(c, up_j))
                r_copy(c, up_j, True).start()

            @pl.when(z > down_j)
            def _():
                pl.when(z < n - 1)(lambda: add_landed(c, down_j))
                r_copy(c, down_j, False).start()
        pl.when(c >= LAG)(lambda: finish(c - LAG))

    pl.loop(outs - LAG, outs)(finish)
    pl.loop(outs - WINDOW, outs)(sent)

    @pl.when(trades)
    def _():
        @pl.loop(0, outs)
        def _(c):
            back(c).wait()
            out_ref[:, pl.ds(pl.multiple_of(c * ow, ow), ow)] = got[c]

    pl.when(early)(lambda: first_half.wait_send())


def on_device(n, seqs, codes, exponents, w_query, w_key, w_value, norm_gain, w_out):
    toks, feats = codes.shape
    depth, width = w_query.shape
    model = w_out.shape[1]
    rows = toks // n
    ow = model // OUT_CHUNKS
    steps = (seqs // 2).bit_length() - 1
    hbm = pl.BlockSpec(memory_space=pl.ANY)
    vmem = pl.BlockSpec(memory_space=pltpu.VMEM)
    dma = pltpu.SemaphoreType.DMA
    return pl.pallas_call(
        functools.partial(kernel, n, seqs),
        out_shape=jax.ShapeDtypeStruct((rows, model), BF),
        in_specs=[hbm, vmem, hbm, hbm, hbm, vmem, hbm],
        out_specs=vmem,
        scratch_shapes=[
            pltpu.VMEM((n, toks, feats), BF),
            pltpu.VMEM((3, depth, width), BF),
            pltpu.VMEM((width, model), BF),
            pltpu.VMEM((3, toks, width), F32),
            pltpu.VMEM((toks, HD), F32),
            pltpu.VMEM((width, HD), F32),
            pltpu.VMEM((width, HD), F32),
            pltpu.VMEM((steps + 1, width, HD), BF),
            pltpu.VMEM((steps + 1, width, HD), BF),
            pltpu.VMEM((OUT_CHUNKS, toks, ow), BF),
            pltpu.VMEM((n + 1, OUT_CHUNKS, rows, ow), BF),
            pltpu.VMEM((OUT_CHUNKS, rows, ow), BF),
            pltpu.VMEM((2, 8, toks), F32),
            pltpu.SemaphoreType.REGULAR,
            dma(()),
            dma((GATHER_CHUNKS,)),
            dma((GATHER_CHUNKS,)),
            dma(()),
            dma(()),
            dma((OUT_CHUNKS,)),
            dma((OUT_CHUNKS,)),
            dma((3, n)),
            dma(()),
            dma((2, n, GATHER_CHUNKS)),
            dma((n, GATHER_CHUNKS)),
            dma((steps + 1,)),
            dma((steps + 1,)),
            dma((n, OUT_CHUNKS)),
            dma((n + 1, OUT_CHUNKS)),
        ],
        compiler_params=pltpu.CompilerParams(
            collective_id=0, has_side_effects=True, vmem_limit_bytes=62 * 1024 * 1024
        ),
        cost_estimate=pl.CostEstimate(
            flops=2 * toks * width * (3 * depth + model) + 4 * toks * toks * width,
            bytes_accessed=2 * (3 * depth * width + width * model),
            transcendentals=2 * toks * width,
        ),
    )(codes, exponents.reshape(1, toks), w_query, w_key, w_value, norm_gain.reshape(1, width), w_out)


def solution(mesh):
    in_specs = (
        P("seq", "tp"), P("seq"), P(None, "tp"), P(None, "tp"), P(None, "tp"), P("tp"), P("tp", None),
    )
    body = functools.partial(on_device, mesh.shape["tp"], mesh.shape["seq"])
    return jax.shard_map(
        body, mesh=mesh, in_specs=in_specs, out_specs=P(("seq", "tp"), None), check_vma=False
    )
```
